256 devices in a mesh: cols: 64 (over x, z, core), lat: 4 (over y).
Axes of the slice: x: 4, y: 4, z: 8, core: 2. Of those that a mesh axis runs over, the one named last changes fastest.
Arguments:
- adjoint: float32 [10, 131072], P(None, ('cols', 'lat')), may hold values from -6 to 6
- impl_tiles: bfloat16 [1024, 7, 128, 128], P(('cols', 'lat')), may hold values from -0.1875 to 0.1875
- expl_tiles: bfloat16 [1024, 7, 128, 128], P(('cols', 'lat')), may hold values from -0.1875 to 0.1875
- impl_dest: int32 [1024, 4], P(('cols', 'lat')), may hold values from 0 to 63, all different within a row; in each aligned block of 4 rows (0 to 3, 4 to 7, ...) at most 2 rows name the same one
- impl_local: int32 [1024, 4], P(('cols', 'lat')), may hold values from 0 to 3
- expl_dest: int32 [1024, 4], P(('cols', 'lat')), may hold values from 0 to 63, all different within a row; in each aligned block of 4 rows (0 to 3, 4 to 7, ...) at most 2 rows name the same one
- expl_local: int32 [1024, 4], P(('cols', 'lat')), may hold values from 0 to 3
- column_depth: int32 [2048], P(('cols', 'lat')), may hold values from 4 to 64
- newton: int32 [2048], P(('cols', 'lat')), may hold values from 2 to 4
- jacobian: bfloat16 [10, 10, 131072], P(None, None, ('cols', 'lat')), may hold values from -0.41 to 0.21
- newton_inverse: bfloat16 [30, 30, 131072], P(None, None, ('cols', 'lat')), may hold values from -0.45 to 1.45
Outputs:
- sensitivity: float32 [10, 131072], P(None, ('cols', 'lat'))
The draws below stay inside these ranges and needn't reach their ends.
Inputs may be any that keep to these rules, and one draw needn't show every extreme that they name: `impl_dest`: the 4 band blocks of a row block have different cols indices; the row blocks of one device name one cols index at most 2 times, and exactly 2 times on some devices. `expl_dest`: as for impl_dest.
All inputs are finite; a program needn't handle non-finite values.
Results may differ from the reference program's by a relative error of at most 0.0056.
Values sent between devices are 32-bit elements; how exact they have to be, the bound alone decides.
No kernel may reach another device: no remote copies, remote signals or barrier semaphores. Data moves between devices by JAX's collectives and lax.ppermute only.
A program may use at most 64 MiB of HBM per device.

```python
import math
import jax
import jax.numpy as jnp
import numpy as np
from jax import lax

TR = 10
SECTIONS = 3
BLK = 128
NBAND = 4
NB = 7
LEV = 64
NEWT = 4
STEPS = 2
RB = 4
CAP = 2
NCB = 1024
NBOX = 131072
NCOL = 2048
N_COLS = 64
N_LAT = 4


def radau_coef_drawn():
    root = math.sqrt(6.0)
    return jnp.array([[(88.0 - 7.0 * root) / 360.0, (296.0 - 169.0 * root) / 1800.0, (-2.0 + 3.0 * root) / 225.0], [(296.0 + 169.0 * root) / 1800.0, (88.0 + 7.0 * root) / 360.0, (-2.0 - 3.0 * root) / 225.0], [(16.0 - root) / 36.0, (16.0 + root) / 36.0, 1.0 / 9.0]], jnp.float32)


def jacobian_parts(key):
    key_off = jax.random.fold_in(key, 101)
    key_perturb = jax.random.fold_in(key, 102)
    key_decay = jax.random.fold_in(key, 103)
    off_diag = jnp.clip(0.05 * jax.random.normal(key_off, (TR, TR, NBOX), jnp.float32), -0.2, 0.2)
    perturb = jnp.clip(0.08 * jax.random.normal(key_perturb, (TR, TR, NBOX), jnp.float32), -0.3, 0.3)
    decay_rate = jnp.exp(jax.random.uniform(key_decay, (TR, NBOX), jnp.float32, math.log(0.05), math.log(0.4)))
    identity = jnp.eye(TR, dtype=jnp.float32)[:, :, None]
    jac_full = off_diag * (1.0 - identity) - identity * decay_rate[:, None, :]
    return (jac_full, perturb)


def draw_jacobian(key, part):
    jac_full, perturb = jacobian_parts(key)
    return jac_full.astype(jnp.bfloat16)


def draw_newton_inverse(key, part):
    jac_full, perturb = jacobian_parts(key)
    approx = jac_full + perturb
    coef = radau_coef_drawn()
    kron_block = coef[:, None, :, None, None] * approx[None, :, None, :, :]
    kron_block = kron_block.reshape(SECTIONS * TR, SECTIONS * TR, NBOX)
    identity = jnp.eye(SECTIONS * TR, dtype=jnp.float32)[:, :, None]
    return (kron_block + identity).astype(jnp.bfloat16)


def plant(drawn, own_key, smallest, high):
    spot = [jax.random.randint(jax.random.fold_in(own_key, axis), (), 0, length) for axis, length in enumerate(drawn.shape)]
    longest = drawn.shape.index(max(drawn.shape))
    next_to = spot[:longest] + [(spot[longest] + 1) % drawn.shape[longest]] + spot[longest + 1:]
    return drawn.at[tuple(spot)].set(smallest).at[tuple(next_to)].set(high)


def block_levels(rng, extent, pieces, least, largest):
    loudness = 1.0
    for position, parts in pieces:
        steps = jax.random.uniform(jax.random.fold_in(jax.random.fold_in(rng, 6), position), (parts,), jnp.float32, least / len(pieces), largest / len(pieces))
        loudness = loudness * jnp.repeat(jnp.exp(steps), extent[position] // parts).reshape((-1,) + (1,) * (len(extent) - 1 - position))
    return loudness


def assign_block(own_key, own, number, rows, count, top, bound, skew):
    sequence = jax.random.permutation(own_key, count)
    crowded, common = shares(count, rows * top, bound, skew, True), shares(count, rows * top, bound, skew, False)
    places = jnp.arange(count)

    def named(tallies, rotation):
        used = int((tallies > 0).sum())
        fixed = max(1, used // 4)
        passed = fixed + (places - fixed + rotation * (used - fixed)) % max(1, count - fixed)
        return jnp.zeros((count,), jnp.int32).at[sequence[jnp.where(places < fixed, places, passed)]].set(jnp.asarray(tallies, jnp.int32))

    tallies = jnp.where(number % 4 == 0, named(crowded, number // 4), named(common, number - number // 4 - 1))
    mixed = jax.random.permutation(jax.random.fold_in(own, 3), count)
    source_of, receiver = mixed[0:count // 2 * 2:2], mixed[1:count // 2 * 2:2]
    margin = jnp.minimum(tallies[source_of] - 1, bound - tallies[receiver]) // 2
    margin = jnp.where((source_of == sequence[0]) | (receiver == sequence[0]) | (tallies[receiver] == 0), 0, jnp.maximum(margin, 0))
    passed = jax.random.randint(jax.random.fold_in(own, 4), (count // 2,), 0, 1 << 20) % (margin + 1)
    tallies = tallies.at[source_of].add(-passed).at[receiver].add(passed)
    members = jnp.searchsorted(jnp.cumsum(tallies), jnp.arange(rows * top), side="right").astype(jnp.int32)
    table = members.reshape(top, rows).T
    table = table[jax.random.permutation(jax.random.fold_in(own, 1), rows)]
    rotation = jax.random.randint(jax.random.fold_in(own, 2), (rows, 1), 0, top)
    return jnp.take_along_axis(table, (jnp.arange(top)[None, :] + rotation) % top, axis=1)


def shares(number_of, total, reach, lean, full):
    weights = [(1 << 20) // math.isqrt(rank ** lean) + 1 for rank in range(1, number_of + 1)]
    largest = reach if full else min(reach, max(-(-total // number_of), total * weights[0] // sum(weights)))
    least = 1 if total - largest >= number_of - 1 else 0
    counts, spare = [largest] + [least] * (number_of - 1), total - largest - least * (number_of - 1)
    while spare > 0:
        movable = [i for i in range(1, number_of) if counts[i] < largest] or [i for i in range(1, number_of) if counts[i] < reach]
        pool, left = sum([weights[i] for i in movable]), spare
        for i in movable:
            extra = min(reach - counts[i], max(1, left * weights[i] // pool), spare)
            counts[i] = counts[i] + extra
            spare = spare - extra
    return np.array(counts)


def centred(own_key, dims, scale, limit, pieces=(), held_as=jnp.bfloat16):
    gain = block_levels(own_key, dims, pieces, -0.22, 0.18) if pieces else 1.0
    values = jax.random.normal(own_key, dims, jnp.float32) * scale * gain
    return jnp.minimum(jnp.maximum(values, -limit), limit).astype(held_as)


def setup_inputs(seed: int = 0) -> dict:
    seeds = jax.random.split(jax.random.key(seed), 12)
    adjoint = centred(seeds[0], (TR, NBOX), 1.0, 6.0, ((1, 256),), jnp.float32)
    impl_tiles = centred(seeds[1], (NCB, NB, BLK, BLK), (BLK * NB) ** -0.5, 0.1875, ((0, 256),))
    expl_tiles = centred(seeds[2], (NCB, NB, BLK, BLK), (BLK * NB) ** -0.5, 0.1875, ((0, 256),))
    impl_dest_keys = jax.random.split(jax.random.fold_in(seeds[3], 1), NCB // RB)
    impl_dest_turns = jax.random.permutation(jax.random.fold_in(seeds[3], 3), NCB // RB)
    impl_dest = jax.vmap(lambda own, number: assign_block(jax.random.fold_in(seeds[3], 2), own, number, RB, N_COLS, NBAND, CAP, 1))(impl_dest_keys, impl_dest_turns).reshape((NCB, NBAND))
    impl_local = plant(jax.random.randint(seeds[4], (NCB, NBAND), 0, RB), jax.random.fold_in(seeds[4], 1), 0, RB - 1).astype(jnp.int32)
    expl_dest_keys = jax.random.split(jax.random.fold_in(seeds[5], 1), NCB // RB)
    expl_dest_turns = jax.random.permutation(jax.random.fold_in(seeds[5], 3), NCB // RB)
    expl_dest = jax.vmap(lambda own, number: assign_block(jax.random.fold_in(seeds[5], 2), own, number, RB, N_COLS, NBAND, CAP, 1))(expl_dest_keys, expl_dest_turns).reshape((NCB, NBAND))
    expl_local = plant(jax.random.randint(seeds[6], (NCB, NBAND), 0, RB), jax.random.fold_in(seeds[6], 1), 0, RB - 1).astype(jnp.int32)
    column_depth = plant(jax.random.randint(seeds[7], (NCOL,), 4, LEV + 1), jax.random.fold_in(seeds[7], 1), 4, LEV).astype(jnp.int32)
    newton = plant(jax.random.randint(seeds[8], (NCOL,), 2, NEWT + 1), jax.random.fold_in(seeds[8], 1), 2, NEWT).astype(jnp.int32)
    jacobian = draw_jacobian(jax.random.fold_in(seeds[11], 71), 0)
    newton_inverse = draw_newton_inverse(jax.random.fold_in(seeds[11], 71), 0)
    return dict(adjoint=adjoint, impl_tiles=impl_tiles, expl_tiles=expl_tiles, impl_dest=impl_dest, impl_local=impl_local, expl_dest=expl_dest, expl_local=expl_local, column_depth=column_depth, newton=newton, jacobian=jacobian, newton_inverse=newton_inverse)


def radau_coef():
    root = math.sqrt(6.0)
    return jnp.array([[(88.0 - 7.0 * root) / 360.0, (296.0 - 169.0 * root) / 1800.0, (-2.0 + 3.0 * root) / 225.0], [(296.0 + 169.0 * root) / 1800.0, (88.0 + 7.0 * root) / 360.0, (-2.0 - 3.0 * root) / 225.0], [(16.0 - root) / 36.0, (16.0 + root) / 36.0, 1.0 / 9.0]], jnp.float32)

def column_adjoint(forcing_in, jacobian, inverse, sweeps):
    highest = lax.Precision.HIGHEST
    coef = radau_coef()
    tracers, boxes = forcing_in.shape
    section_count = inverse.shape[0] // tracers
    jac_float = jacobian.astype(jnp.float32)
    inverse_float = inverse.astype(jnp.float32)
    forcing = jnp.zeros((section_count, tracers, boxes), jnp.float32).at[section_count - 1].set(forcing_in)
    sections = jnp.zeros((section_count, tracers, boxes), jnp.float32)
    for sweep in range(NEWT):
        mixed_term = jnp.einsum('ijb,sib->sjb', jac_float, sections, precision=highest)
        image_term = sections - jnp.einsum('rs,rjb->sjb', coef, mixed_term, precision=highest)
        residual = (forcing - image_term).reshape(section_count * tracers, boxes)
        update = jnp.einsum('qpb,qb->pb', inverse_float, residual, precision=highest)
        sections = jnp.where(sweep < sweeps, sections + update.reshape(section_count, tracers, boxes), sections)
    return lax.optimization_barrier(jnp.sum(sections, axis=0))

def block_targets(dest, local):
    block_total = RB * N_COLS * N_LAT
    block_ids = jnp.arange(block_total, dtype=jnp.int32)
    owner = block_ids // RB
    lat_index = owner % N_LAT
    band_target = ((dest * N_LAT + lat_index[:, None]) * RB + local).astype(jnp.int32)
    north_target = jnp.where(lat_index + 1 < N_LAT, block_ids + RB, block_total).astype(jnp.int32)
    south_target = jnp.where(lat_index > 0, block_ids - RB, block_total).astype(jnp.int32)
    return jnp.concatenate([block_ids[:, None], band_target, north_target[:, None], south_target[:, None]], axis=1)

def transport_transpose(field, tiles, targets):
    highest = lax.Precision.HIGHEST
    devices = N_COLS * N_LAT
    block_total = RB * devices
    field_bf = field.astype(jnp.bfloat16).reshape(TR, devices, RB, BLK).transpose(1, 0, 2, 3)
    grouped_tiles = tiles.reshape(devices, RB, NB, BLK, BLK)

    def one_group(pair):
        return jnp.einsum('cri,rtij->rtcj', pair[0].astype(jnp.float32), pair[1].astype(jnp.float32), precision=highest)
    terms_all = lax.map(one_group, (field_bf, grouped_tiles))
    flattened = terms_all.reshape(block_total * NB, TR * BLK)
    summed = jax.ops.segment_sum(flattened, targets.reshape(-1), num_segments=block_total + 1)[:block_total]
    return summed.reshape(block_total, TR, BLK).transpose(1, 0, 2).reshape(TR, block_total * BLK)

def reference(adjoint, impl_tiles, expl_tiles, impl_dest, impl_local, expl_dest, expl_local, column_depth, newton, jacobian, newton_inverse):
    devices = N_COLS * N_LAT
    boxes = RB * BLK
    levels = jnp.arange(LEV, dtype=jnp.int32)
    wet_mask = (levels[None, :] < column_depth[:, None]).astype(jnp.float32).reshape(-1)
    sweeps = jnp.broadcast_to(newton[:, None], (newton.shape[0], LEV)).reshape(-1)
    impl_targets = block_targets(impl_dest, impl_local)
    expl_targets = block_targets(expl_dest, expl_local)

    def chemistry(field):

        def one_group(group):
            start = group * boxes
            return column_adjoint(lax.dynamic_slice_in_dim(field, start, boxes, 1), lax.dynamic_slice_in_dim(jacobian, start, boxes, 2), lax.dynamic_slice_in_dim(newton_inverse, start, boxes, 2), lax.dynamic_slice_in_dim(sweeps, start, boxes, 0))
        result = lax.map(one_group, jnp.arange(devices, dtype=jnp.int32))
        return result.transpose(1, 0, 2).reshape(TR, devices * boxes)
    adjoint_now = adjoint
    for step_index in range(STEPS):
        transported = wet_mask * transport_transpose(adjoint_now, impl_tiles, impl_targets)
        reacted = chemistry(transported)
        adjoint_now = wet_mask * transport_transpose(reacted, expl_tiles, expl_targets)
    return adjoint_now
```

```python
import math

import jax
import jax.numpy as jnp
from jax import lax
from jax.experimental import pallas as pl
from jax.experimental.pallas import tpu as pltpu
from jax.sharding import PartitionSpec as P

NEWT = 4
STEPS = 2
TR = 10
SECTIONS = 3
BLK = 128
NBAND = 4
NB = 7
LEV = 64
RB = 4
NX, NZ, NCORE = 4, 8, 2
N_LAT = 4
TERMS = RB * NBAND
SLAB = RB * TR
F32 = jnp.float32

ROOT = math.sqrt(6.0)
COEF = [
    [(88.0 - 7.0 * ROOT) / 360.0, (296.0 - 169.0 * ROOT) / 1800.0, (-2.0 + 3.0 * ROOT) / 225.0],
    [(296.0 + 169.0 * ROOT) / 1800.0, (88.0 + 7.0 * ROOT) / 360.0, (-2.0 - 3.0 * ROOT) / 225.0],
    [(16.0 - ROOT) / 36.0, (16.0 + ROOT) / 36.0, 1.0 / 9.0],
]

VMEM = pl.BlockSpec(memory_space=pltpu.VMEM)
SMEM = pl.BlockSpec(memory_space=pltpu.SMEM)


def cols_id(x, z, core):
    return (x * NZ + z) * NCORE + core


def shift_x(value, steps):
    pairs = [
        (cols_id(x, z, c), cols_id((x + steps) % NX, z, c))
        for x in range(NX)
        for z in range(NZ)
        for c in range(NCORE)
    ]
    return lax.ppermute(value, "cols", pairs)


def swap_core(value):
    return lax.ppermute(value, "cols", [(i, i ^ 1) for i in range(NX * NZ * NCORE)])


def ring_lat(value, steps):
    return lax.ppermute(value, "lat", [(i, (i + steps) % N_LAT) for i in range(N_LAT)])


def exchange_z(value):
    groups = [[cols_id(x, z, c) for z in range(NZ)] for x in range(NX) for c in range(NCORE)]
    return lax.all_to_all(value, "cols", 0, 0, axis_index_groups=groups, tiled=True)


def emit_terms(blocks, tiles_ref, raw_ref, own_ref, north_ref, south_ref):
    for r in range(RB):
        padded = jnp.concatenate([blocks[r], jnp.zeros((16 - TR, BLK), F32)], axis=0)
        left = padded.astype(jnp.bfloat16)
        for t in range(NB):
            term = jnp.dot(left, tiles_ref[r, t], preferred_element_type=F32)[:TR]
            if t == 0:
                own_ref[r * TR : (r + 1) * TR, :] = term
            elif t <= NBAND:
                k = r * NBAND + t - 1
                raw_ref[k * TR : (k + 1) * TR, :] = term
            elif t == NBAND + 1:
                north_ref[r * TR : (r + 1) * TR, :] = term
            else:
                south_ref[r * TR : (r + 1) * TR, :] = term


def first_kernel(field_ref, tiles_ref, raw_ref, own_ref, north_ref, south_ref):
    blocks = [field_ref[:, r * BLK : (r + 1) * BLK] for r in range(RB)]
    emit_terms(blocks, tiles_ref, raw_ref, own_ref, north_ref, south_ref)


def merge_kernel(slot_ref, raw0, raw1, raw2, raw3, mine_ref, other_ref, acc):
    acc[...] = jnp.zeros_like(acc)
    for source, raw in enumerate((raw0, raw1, raw2, raw3)):
        for k in range(TERMS):
            slot = slot_ref[source, k]
            acc[slot] = acc[slot] + raw[k * TR : (k + 1) * TR, :]
    for slot in range(NZ * RB):
        mine_ref[slot * TR : (slot + 1) * TR, :] = acc[slot]
        other_ref[slot * TR : (slot + 1) * TR, :] = acc[NZ * RB + slot]


def arrived_blocks(edge_ref, slabs_ref, own_ref, below_ref, above_ref, wet_ref):
    total = own_ref[...]
    for z in range(NZ):
        total = total + slabs_ref[z]
    total = total + jnp.where(edge_ref[0] > 0, below_ref[...], 0.0)
    total = total + jnp.where(edge_ref[1] > 0, above_ref[...], 0.0)
    return [total[r * TR : (r + 1) * TR, :] * wet_ref[r : r + 1, :] for r in range(RB)]


def column_block(forcing, r, jac_ref, inv_ref, sweeps):
    lanes = slice(r * BLK, (r + 1) * BLK)

    def image_update(rows):
        total = None
        for q, row in rows:
            part = inv_ref[q, :, lanes].astype(F32) * row
            total = part if total is None else total + part
        return total

    rows = [(2 * TR + i, forcing[i : i + 1, :]) for i in range(TR)]
    update = jnp.where(0 < sweeps, image_update(rows), 0.0)
    z = [update[s * TR : (s + 1) * TR, :] for s in range(SECTIONS)]
    for sweep in range(1, NEWT):
        mixed = [None] * SECTIONS
        for i in range(TR):
            jac = jac_ref[i, :, lanes].astype(F32)
            for s in range(SECTIONS):
                part = jac * z[s][i : i + 1, :]
                mixed[s] = part if mixed[s] is None else mixed[s] + part
        rows = []
        for s in range(SECTIONS):
            mix = COEF[0][s] * mixed[0] + COEF[1][s] * mixed[1] + COEF[2][s] * mixed[2]
            residual = mix - z[s]
            if s == SECTIONS - 1:
                residual = residual + forcing
            rows += [(s * TR + i, residual[i : i + 1, :]) for i in range(TR)]
        update = jnp.where(sweep < sweeps, image_update(rows), 0.0)
        z = [z[s] + update[s * TR : (s + 1) * TR, :] for s in range(SECTIONS)]
    return z[0] + z[1] + z[2]


def react_kernel(
    edge_ref, slabs_ref, own_in, below_ref, above_ref, wet_ref, sweeps_ref, jac_ref, inv_ref,
    tiles_ref, raw_ref, own_ref, north_ref, south_ref,
):
    blocks = arrived_blocks(edge_ref, slabs_ref, own_in, below_ref, above_ref, wet_ref)
    blocks = [
        column_block(blocks[r], r, jac_ref, inv_ref, sweeps_ref[r : r + 1, :]) for r in range(RB)
    ]
    emit_terms(blocks, tiles_ref, raw_ref, own_ref, north_ref, south_ref)


def step_kernel(
    edge_ref, slabs_ref, own_in, below_ref, above_ref, wet_ref,
    tiles_ref, raw_ref, own_ref, north_ref, south_ref,
):
    blocks = arrived_blocks(edge_ref, slabs_ref, own_in, below_ref, above_ref, wet_ref)
    emit_terms(blocks, tiles_ref, raw_ref, own_ref, north_ref, south_ref)


def last_kernel(edge_ref, slabs_ref, own_in, below_ref, above_ref, wet_ref, out_ref):
    blocks = arrived_blocks(edge_ref, slabs_ref, own_in, below_ref, above_ref, wet_ref)
    for r in range(RB):
        out_ref[:, r * BLK : (r + 1) * BLK] = blocks[r]


def struct(*shape):
    return jax.ShapeDtypeStruct(shape, F32)


TERM_SHAPES = (
    struct(TERMS * TR, BLK),
    struct(SLAB, BLK),
    struct(SLAB, BLK),
    struct(SLAB, BLK),
)


def call(kernel, out_shape, operands, smem, name, scratch=(), flops=0):
    many = isinstance(out_shape, tuple)
    size = sum(a.size * a.dtype.itemsize for a in operands)
    return pl.pallas_call(
        kernel,
        out_shape=out_shape,
        in_specs=[SMEM] * smem + [VMEM] * (len(operands) - smem),
        out_specs=[VMEM] * len(out_shape) if many else VMEM,
        scratch_shapes=scratch,
        compiler_params=pltpu.CompilerParams(vmem_limit_bytes=32 * 1024 * 1024),
        cost_estimate=pl.CostEstimate(flops=flops, bytes_accessed=size, transcendentals=0),
        name=name,
    )(*operands)


def body(
    adjoint,
    impl_tiles,
    expl_tiles,
    impl_dest,
    impl_local,
    expl_dest,
    expl_local,
    column_depth,
    newton,
    jacobian,
    newton_inverse,
):
    cols = lax.axis_index("cols")
    lat = lax.axis_index("lat")
    my_x = cols // (NZ * NCORE)
    my_core = cols % NCORE
    edges = jnp.stack([lat > 0, lat < N_LAT - 1]).astype(jnp.int32)

    codes = jnp.stack([impl_dest * RB + impl_local, expl_dest * RB + expl_local])
    codes = codes.reshape(2, TERMS)
    gathered = jnp.stack([codes] + [shift_x(codes, k) for k in range(1, NX)], axis=1)
    owner, local = gathered // RB, gathered % RB
    place = (owner // NCORE) % NZ * RB + local
    place = place + jnp.where(owner % NCORE == my_core, 0, NZ * RB)
    slots = jnp.where(owner // (NZ * NCORE) == my_x, place, 2 * NZ * RB).astype(jnp.int32)

    level = jnp.arange(LEV, dtype=jnp.int32)
    wet = (level[None, :] < column_depth[:, None]).astype(F32).reshape(RB, BLK)
    sweeps = jnp.broadcast_to(newton[:, None], (newton.shape[0], LEV)).reshape(RB, BLK)

    def deliver(terms, slot):
        raw, own, north, south = terms
        raws = [raw] + [shift_x(raw, k) for k in range(1, NX)]
        mine, other = call(
            merge_kernel,
            (struct(NZ * SLAB, BLK), struct(NZ * SLAB, BLK)),
            [slot] + raws,
            1,
            "merge",
            [pltpu.VMEM((2 * NZ * RB + 1, TR, BLK), F32)],
        )
        dense = (mine + swap_core(other)).reshape(NZ, SLAB, BLK)
        slabs = exchange_z(dense)
        return [edges, slabs, own, ring_lat(north, 1), ring_lat(south, N_LAT - 1), wet]

    terms = call(first_kernel, TERM_SHAPES, [adjoint, impl_tiles], 0, "first")
    for step_index in range(STEPS):
        arrived = deliver(terms, slots[0])
        terms = call(
            react_kernel,
            TERM_SHAPES,
            arrived + [sweeps, jacobian, newton_inverse, expl_tiles],
            1,
            "react",
        )
        arrived = deliver(terms, slots[1])
        if step_index + 1 < STEPS:
            terms = call(step_kernel, TERM_SHAPES, arrived + [impl_tiles], 1, "step")
    return call(last_kernel, struct(TR, RB * BLK), arrived, 1, "last")


def solution(mesh):
    both = ("cols", "lat")
    return jax.shard_map(
        body,
        mesh=mesh,
        in_specs=(
            P(None, both),
            P(both, None, None, None),
            P(both, None, None, None),
            P(both, None),
            P(both, None),
            P(both, None),
            P(both, None),
            P(both),
            P(both),
            P(None, None, both),
            P(None, None, both),
        ),
        out_specs=P(None, both),
        check_vma=False,
    )
```

```python
import math

import jax
import jax.numpy as jnp
from jax import lax
from jax.experimental import pallas as pl
from jax.experimental.pallas import tpu as pltpu
from jax.sharding import PartitionSpec as P

NEWT = 4
STEPS = 2
TR = 10
SECTIONS = 3
BLK = 128
NBAND = 4
NB = 7
LEV = 64
RB = 4
NX, NZ, NCORE = 4, 8, 2
N_LAT = 4
TERMS = RB * NBAND
SLAB = RB * TR
F32 = jnp.float32

ROOT = math.sqrt(6.0)
COEF = [
    [(88.0 - 7.0 * ROOT) / 360.0, (296.0 - 169.0 * ROOT) / 1800.0, (-2.0 + 3.0 * ROOT) / 225.0],
    [(296.0 + 169.0 * ROOT) / 1800.0, (88.0 + 7.0 * ROOT) / 360.0, (-2.0 - 3.0 * ROOT) / 225.0],
    [(16.0 - ROOT) / 36.0, (16.0 + ROOT) / 36.0, 1.0 / 9.0],
]

VMEM = pl.BlockSpec(memory_space=pltpu.VMEM)
SMEM = pl.BlockSpec(memory_space=pltpu.SMEM)
FAR = pl.BlockSpec(memory_space=pltpu.HBM)


def cols_id(x, z, core):
    return (x * NZ + z) * NCORE + core


def shift_x(value, steps):
    pairs = [
        (cols_id(x, z, c), cols_id((x + steps) % NX, z, c))
        for x in range(NX)
        for z in range(NZ)
        for c in range(NCORE)
    ]
    return lax.ppermute(value, "cols", pairs)


def swap_core(value):
    return lax.ppermute(value, "cols", [(i, i ^ 1) for i in range(NX * NZ * NCORE)])


def ring_lat(value, steps):
    return lax.ppermute(value, "lat", [(i, (i + steps) % N_LAT) for i in range(N_LAT)])


def exchange_z(value):
    groups = [[cols_id(x, z, c) for z in range(NZ)] for x in range(NX) for c in range(NCORE)]
    return lax.all_to_all(value, "cols", 0, 0, axis_index_groups=groups, tiled=True)


def emit_terms(blocks, tiles_ref, raw_ref, own_ref, north_ref, south_ref, ready=None):
    for r in range(RB):
        if ready is not None:
            ready[r].wait()
        padded = jnp.concatenate([blocks[r], jnp.zeros((16 - TR, BLK), F32)], axis=0)
        left = padded.astype(jnp.bfloat16)
        for t in range(NB):
            term = jnp.dot(left, tiles_ref[r, t], preferred_element_type=F32)[:TR]
            if t == 0:
                own_ref[r * TR : (r + 1) * TR, :] = term
            elif t <= NBAND:
                k = r * NBAND + t - 1
                raw_ref[k * TR : (k + 1) * TR, :] = term
            elif t == NBAND + 1:
                north_ref[r * TR : (r + 1) * TR, :] = term
            else:
                south_ref[r * TR : (r + 1) * TR, :] = term


def first_kernel(
    field_far, impl_dest_far, impl_local_far, expl_dest_far, expl_local_far, tiles_far,
    raw_ref, own_ref, north_ref, south_ref,
    field_ref, impl_dest, impl_local, expl_dest, expl_local, tiles_ref, arrivals, tile_arrivals,
):
    copies = [
        pltpu.make_async_copy(far, near, arrivals.at[i])
        for i, (far, near) in enumerate(
            (
                (field_far, field_ref),
                (impl_dest_far, impl_dest),
                (impl_local_far, impl_local),
                (expl_dest_far, expl_dest),
                (expl_local_far, expl_local),
            )
        )
    ]
    tile_copies = [
        pltpu.make_async_copy(tiles_far.at[r], tiles_ref.at[r], tile_arrivals.at[r])
        for r in range(RB)
    ]
    for copy in copies + tile_copies:
        copy.start()
    raw_ref[TERMS * TR :, :] = jnp.zeros((2 * RB, BLK), F32)
    for copy in copies:
        copy.wait()
    impl_codes = impl_dest[...] * RB + impl_local[...]
    expl_codes = expl_dest[...] * RB + expl_local[...]
    raw_ref[TERMS * TR : TERMS * TR + RB, :NBAND] = impl_codes.astype(F32)
    raw_ref[TERMS * TR + RB :, :NBAND] = expl_codes.astype(F32)
    blocks = [field_ref[:, r * BLK : (r + 1) * BLK] for r in range(RB)]
    emit_terms(blocks, tiles_ref, raw_ref, own_ref, north_ref, south_ref, tile_copies)


def slots_kernel(raw0, raw1, raw2, raw3, impl_ref, expl_ref):
    cols = lax.axis_index("cols")
    my_core = cols & (NCORE - 1)
    my_x = cols // (NZ * NCORE)
    for source, raw in enumerate((raw0, raw1, raw2, raw3)):
        codes = raw[TERMS * TR :, :].astype(jnp.int32)
        owner, local = codes // RB, codes & (RB - 1)
        place = ((owner // NCORE) & (NZ - 1)) * RB + local
        place = place + jnp.where((owner & (NCORE - 1)) == my_core, 0, NZ * RB)
        slot = jnp.where(owner // (NZ * NCORE) == my_x, place, 2 * NZ * RB)
        impl_ref[source * RB : (source + 1) * RB, :] = slot[:RB, :NBAND]
        expl_ref[source * RB : (source + 1) * RB, :] = slot[RB:, :NBAND]


def masks_kernel(depth_ref, newton_ref, mask_ref, sweeps_ref):
    lat = lax.axis_index("lat")
    lane = lax.broadcasted_iota(jnp.int32, (1, BLK), 1)
    first = lane < LEV
    level = jnp.where(first, lane, lane - LEV)
    for r in range(RB):
        depth = jnp.where(first, depth_ref[2 * r], depth_ref[2 * r + 1])
        mask_ref[r : r + 1, :] = jnp.where(level < depth, 1.0, 0.0)
        sweeps_ref[r : r + 1, :] = jnp.where(first, newton_ref[2 * r], newton_ref[2 * r + 1])
    mask_ref[RB : RB + 1, :] = jnp.where(lane * 0 + lat > 0, 1.0, 0.0)
    mask_ref[RB + 1 : RB + 2, :] = jnp.where(lane * 0 + lat < N_LAT - 1, 1.0, 0.0)


def merge_kernel(slot_ref, raw0, raw1, raw2, raw3, mine_ref, other_ref, acc0, acc1):
    acc0[...] = jnp.zeros_like(acc0)
    acc1[...] = jnp.zeros_like(acc1)
    for pair in (((0, raw0, acc0), (1, raw1, acc1)), ((2, raw2, acc0), (3, raw3, acc1))):
        for k in range(TERMS):
            for source, raw, acc in pair:
                slot = slot_ref[source * RB + k // NBAND, k % NBAND]
                acc[slot] = acc[slot] + raw[k * TR : (k + 1) * TR, :]
    for slot in range(NZ * RB):
        mine_ref[slot * TR : (slot + 1) * TR, :] = acc0[slot] + acc1[slot]
        far = NZ * RB + slot
        other_ref[slot * TR : (slot + 1) * TR, :] = acc0[far] + acc1[far]


def arrived_blocks(mask_ref, slabs_ref, own_ref, below_ref, above_ref):
    total = own_ref[...] + below_ref[...] * mask_ref[RB : RB + 1, :]
    total = total + above_ref[...] * mask_ref[RB + 1 : RB + 2, :]
    for z in range(NZ):
        total = total + slabs_ref[z]
    return [total[r * TR : (r + 1) * TR, :] * mask_ref[r : r + 1, :] for r in range(RB)]


def column_block(forcing, r, jac_ref, inv_ref, sweeps):
    lanes = slice(r * BLK, (r + 1) * BLK)

    def image_update(rows):
        total = None
        for q, row in rows:
            part = inv_ref[q, :, lanes].astype(F32) * row
            total = part if total is None else total + part
        return total

    rows = [(2 * TR + i, forcing[i : i + 1, :]) for i in range(TR)]
    update = jnp.where(0 < sweeps, image_update(rows), 0.0)
    z = [update[s * TR : (s + 1) * TR, :] for s in range(SECTIONS)]
    for sweep in range(1, NEWT):
        mixed = [None] * SECTIONS
        for i in range(TR):
            jac = jac_ref[i, :, lanes].astype(F32)
            for s in range(SECTIONS):
                part = jac * z[s][i : i + 1, :]
                mixed[s] = part if mixed[s] is None else mixed[s] + part
        rows = []
        for s in range(SECTIONS):
            mix = COEF[0][s] * mixed[0] + COEF[1][s] * mixed[1] + COEF[2][s] * mixed[2]
            residual = mix - z[s]
            if s == SECTIONS - 1:
                residual = residual + forcing
            rows += [(s * TR + i, residual[i : i + 1, :]) for i in range(TR)]
        update = jnp.where(sweep < sweeps, image_update(rows), 0.0)
        z = [z[s] + update[s * TR : (s + 1) * TR, :] for s in range(SECTIONS)]
    return z[0] + z[1] + z[2]


def react_kernel(
    mask_ref, slabs_ref, own_in, below_ref, above_ref, sweeps_ref, jac_ref, inv_ref,
    tiles_ref, raw_ref, own_ref, north_ref, south_ref,
):
    blocks = arrived_blocks(mask_ref, slabs_ref, own_in, below_ref, above_ref)
    blocks = [
        column_block(blocks[r], r, jac_ref, inv_ref, sweeps_ref[r : r + 1, :]) for r in range(RB)
    ]
    emit_terms(blocks, tiles_ref, raw_ref, own_ref, north_ref, south_ref)


def step_kernel(
    mask_ref, slabs_ref, own_in, below_ref, above_ref,
    tiles_ref, raw_ref, own_ref, north_ref, south_ref,
):
    blocks = arrived_blocks(mask_ref, slabs_ref, own_in, below_ref, above_ref)
    emit_terms(blocks, tiles_ref, raw_ref, own_ref, north_ref, south_ref)


def last_kernel(mask_ref, slabs_ref, own_in, below_ref, above_ref, out_ref):
    blocks = arrived_blocks(mask_ref, slabs_ref, own_in, below_ref, above_ref)
    for r in range(RB):
        out_ref[:, r * BLK : (r + 1) * BLK] = blocks[r]


def struct(*shape):
    return jax.ShapeDtypeStruct(shape, F32)


TERM_SHAPES = (
    struct(TERMS * TR, BLK),
    struct(SLAB, BLK),
    struct(SLAB, BLK),
    struct(SLAB, BLK),
)


def call(kernel, out_shape, operands, smem, name, far=0, scratch=(), vmem_mib=12):
    many = isinstance(out_shape, tuple)
    size = sum(a.size * a.dtype.itemsize for a in operands)
    return pl.pallas_call(
        kernel,
        out_shape=out_shape,
        in_specs=[SMEM] * smem + [VMEM] * (len(operands) - smem - far) + [FAR] * far,
        out_specs=[VMEM] * len(out_shape) if many else VMEM,
        scratch_shapes=scratch,
        compiler_params=pltpu.CompilerParams(vmem_limit_bytes=vmem_mib * 1024 * 1024),
        cost_estimate=pl.CostEstimate(flops=0, bytes_accessed=size, transcendentals=0),
        name=name,
    )(*operands)


def body(
    adjoint,
    impl_tiles,
    expl_tiles,
    impl_dest,
    impl_local,
    expl_dest,
    expl_local,
    column_depth,
    newton,
    jacobian,
    newton_inverse,
):
    def gather_x(raw):
        return [shift_x(raw, k) for k in range(1, NX)]

    def deliver(terms, raws, slot):
        raw, own, north, south = terms
        dense = struct(NZ * SLAB, BLK)
        acc = pltpu.VMEM((2 * NZ * RB + 1, TR, BLK), F32)
        mine, other = call(
            merge_kernel, (dense, dense), [slot, raw, *raws], 1, "merge", scratch=[acc, acc]
        )
        slabs = exchange_z((mine + swap_core(other)).reshape(NZ, SLAB, BLK))
        return [masks, slabs, own, ring_lat(north, 1), ring_lat(south, N_LAT - 1)]

    int_table = jax.ShapeDtypeStruct((RB, BLK), jnp.int32)
    masks, sweeps = call(
        masks_kernel, (struct(RB + 2, BLK), int_table), [column_depth, newton], 2, "masks"
    )
    first_shapes = (struct(TERMS * TR + 2 * RB, BLK),) + TERM_SHAPES[1:]
    terms = call(
        first_kernel,
        first_shapes,
        [adjoint, impl_dest, impl_local, expl_dest, expl_local, impl_tiles],
        0,
        "first",
        far=6,
        vmem_mib=63,
        scratch=[
            pltpu.VMEM((TR, RB * BLK), F32),
            *[pltpu.VMEM((RB, NBAND), jnp.int32)] * 4,
            pltpu.VMEM((RB, NB, BLK, BLK), jnp.bfloat16),
            pltpu.SemaphoreType.DMA((5,)),
            pltpu.SemaphoreType.DMA((RB,)),
        ],
    )
    raws = gather_x(terms[0])
    slot_table = jax.ShapeDtypeStruct((NX * RB, NBAND), jnp.int32)
    slots = call(slots_kernel, (slot_table, slot_table), [terms[0], *raws], 0, "slots")
    for step_index in range(STEPS):
        if step_index:
            raws = gather_x(terms[0])
        arrived = deliver(terms, raws, slots[0])
        terms = call(
            react_kernel,
            TERM_SHAPES,
            arrived + [sweeps, jacobian, newton_inverse, expl_tiles],
            0,
            "react",
        )
        arrived = deliver(terms, gather_x(terms[0]), slots[1])
        if step_index + 1 < STEPS:
            terms = call(step_kernel, TERM_SHAPES, arrived + [impl_tiles], 0, "step")
    return call(last_kernel, struct(TR, RB * BLK), arrived, 0, "last")


def solution(mesh):
    both = ("cols", "lat")
    return jax.shard_map(
        body,
        mesh=mesh,
        in_specs=(
            P(None, both),
            P(both, None, None, None),
            P(both, None, None, None),
            P(both, None),
            P(both, None),
            P(both, None),
            P(both, None),
            P(both),
            P(both),
            P(None, None, both),
            P(None, None, both),
        ),
        out_specs=P(None, both),
        check_vma=False,
    )
```

```python
import math

import jax
import jax.numpy as jnp
from jax import lax
from jax.experimental import pallas as pl
from jax.experimental.pallas import tpu as pltpu
from jax.sharding import PartitionSpec as P

NEWT = 4
STEPS = 2
TR = 10
SECTIONS = 3
BLK = 128
NBAND = 4
NB = 7
LEV = 64
RB = 4
NX, NZ, NCORE = 4, 8, 2
N_LAT = 4
TERMS = RB * NBAND
SLAB = RB * TR
F32 = jnp.float32

ROOT = math.sqrt(6.0)
COEF = [
    [(88.0 - 7.0 * ROOT) / 360.0, (296.0 - 169.0 * ROOT) / 1800.0, (-2.0 + 3.0 * ROOT) / 225.0],
    [(296.0 + 169.0 * ROOT) / 1800.0, (88.0 + 7.0 * ROOT) / 360.0, (-2.0 - 3.0 * ROOT) / 225.0],
    [(16.0 - ROOT) / 36.0, (16.0 + ROOT) / 36.0, 1.0 / 9.0],
]

VMEM = pl.BlockSpec(memory_space=pltpu.VMEM)
SMEM = pl.BlockSpec(memory_space=pltpu.SMEM)
FAR = pl.BlockSpec(memory_space=pltpu.HBM)


def cols_id(x, z, core):
    return (x * NZ + z) * NCORE + core


def shift_x(value, steps):
    pairs = [
        (cols_id(x, z, c), cols_id((x + steps) % NX, z, c))
        for x in range(NX)
        for z in range(NZ)
        for c in range(NCORE)
    ]
    return lax.ppermute(value, "cols", pairs)


def swap_core(value):
    return lax.ppermute(value, "cols", [(i, i ^ 1) for i in range(NX * NZ * NCORE)])


def ring_lat(value, steps):
    return lax.ppermute(value, "lat", [(i, (i + steps) % N_LAT) for i in range(N_LAT)])


def exchange_z(value):
    groups = [[cols_id(x, z, c) for z in range(NZ)] for x in range(NX) for c in range(NCORE)]
    return lax.all_to_all(value, "cols", 0, 0, axis_index_groups=groups, tiled=True)


def emit_terms(blocks, tiles_ref, raw_ref, own_ref, north_ref, south_ref, ready=None):
    for r in range(RB):
        if ready is not None:
            ready[r].wait()
        padded = jnp.concatenate([blocks[r], jnp.zeros((16 - TR, BLK), F32)], axis=0)
        left = padded.astype(jnp.bfloat16)
        for t in range(NB):
            term = jnp.dot(left, tiles_ref[r, t], preferred_element_type=F32)[:TR]
            if t == 0:
                own_ref[r * TR : (r + 1) * TR, :] = term
            elif t <= NBAND:
                k = r * NBAND + t - 1
                raw_ref[k * TR : (k + 1) * TR, :] = term
            elif t == NBAND + 1:
                north_ref[r * TR : (r + 1) * TR, :] = term
            else:
                south_ref[r * TR : (r + 1) * TR, :] = term


def first_kernel(
    field_far, impl_dest_far, impl_local_far, expl_dest_far, expl_local_far, tiles_far,
    raw_ref, own_ref, north_ref, south_ref,
    field_ref, impl_dest, impl_local, expl_dest, expl_local, tiles_ref, arrivals, tile_arrivals,
):
    copies = [
        pltpu.make_async_copy(far, near, arrivals.at[i])
        for i, (far, near) in enumerate(
            (
                (field_far, field_ref),
                (impl_dest_far, impl_dest),
                (impl_local_far, impl_local),
                (expl_dest_far, expl_dest),
                (expl_local_far, expl_local),
            )
        )
    ]
    tile_copies = [
        pltpu.make_async_copy(tiles_far.at[r], tiles_ref.at[r], tile_arrivals.at[r])
        for r in range(RB)
    ]
    for copy in copies + tile_copies:
        copy.start()
    raw_ref[TERMS * TR :, :] = jnp.zeros((2 * RB, BLK), F32)
    for copy in copies:
        copy.wait()
    impl_codes = impl_dest[...] * RB + impl_local[...]
    expl_codes = expl_dest[...] * RB + expl_local[...]
    raw_ref[TERMS * TR : TERMS * TR + RB, :NBAND] = impl_codes.astype(F32)
    raw_ref[TERMS * TR + RB :, :NBAND] = expl_codes.astype(F32)
    blocks = [field_ref[:, r * BLK : (r + 1) * BLK] for r in range(RB)]
    emit_terms(blocks, tiles_ref, raw_ref, own_ref, north_ref, south_ref, tile_copies)


def slots_kernel(raw0, raw1, raw2, raw3, impl_ref, expl_ref):
    cols = lax.axis_index("cols")
    my_core = cols & (NCORE - 1)
    my_x = cols // (NZ * NCORE)
    for source, raw in enumerate((raw0, raw1, raw2, raw3)):
        codes = raw[TERMS * TR :, :].astype(jnp.int32)
        owner, local = codes // RB, codes & (RB - 1)
        place = ((owner // NCORE) & (NZ - 1)) * RB + local
        place = place + jnp.where((owner & (NCORE - 1)) == my_core, 0, NZ * RB)
        slot = jnp.where(owner // (NZ * NCORE) == my_x, place, 2 * NZ * RB)
        impl_ref[source * RB : (source + 1) * RB, :] = slot[:RB, :NBAND]
        expl_ref[source * RB : (source + 1) * RB, :] = slot[RB:, :NBAND]


def masks_kernel(depth_ref, newton_ref, mask_ref, sweeps_ref):
    lat = lax.axis_index("lat")
    lane = lax.broadcasted_iota(jnp.int32, (1, BLK), 1)
    first = lane < LEV
    level = jnp.where(first, lane, lane - LEV)
    for r in range(RB):
        depth = jnp.where(first, depth_ref[2 * r], depth_ref[2 * r + 1])
        mask_ref[r : r + 1, :] = jnp.where(level < depth, 1.0, 0.0)
        sweeps_ref[r : r + 1, :] = jnp.where(first, newton_ref[2 * r], newton_ref[2 * r + 1])
    mask_ref[RB : RB + 1, :] = jnp.where(lane * 0 + lat > 0, 1.0, 0.0)
    mask_ref[RB + 1 : RB + 2, :] = jnp.where(lane * 0 + lat < N_LAT - 1, 1.0, 0.0)


def merge_kernel(slot_ref, raw0, raw1, raw2, raw3, mine_ref, other_ref, acc0, acc1):
    acc0[...] = jnp.zeros_like(acc0)
    acc1[...] = jnp.zeros_like(acc1)
    slots = slot_ref[...]
    for pair in (((0, raw0, acc0), (1, raw1, acc1)), ((2, raw2, acc0), (3, raw3, acc1))):
        for k in range(TERMS):
            for source, raw, acc in pair:
                slot = slots[source * RB + k // NBAND, k % NBAND]
                acc[slot] = acc[slot] + raw[k * TR : (k + 1) * TR, :]
    for slot in range(NZ * RB):
        mine_ref[slot * TR : (slot + 1) * TR, :] = acc0[slot] + acc1[slot]
        far = NZ * RB + slot
        other_ref[slot * TR : (slot + 1) * TR, :] = acc0[far] + acc1[far]


def arrived_blocks(mask_ref, slabs_ref, own_ref, below_ref, above_ref):
    total = own_ref[...] + below_ref[...] * mask_ref[RB : RB + 1, :]
    total = total + above_ref[...] * mask_ref[RB + 1 : RB + 2, :]
    for z in range(NZ):
        total = total + slabs_ref[z]
    return [total[r * TR : (r + 1) * TR, :] * mask_ref[r : r + 1, :] for r in range(RB)]


def column_block(forcing, r, jac_ref, inv_ref, sweeps):
    lanes = slice(r * BLK, (r + 1) * BLK)

    def image_update(rows):
        total = None
        for q, row in rows:
            part = inv_ref[q, :, lanes].astype(F32) * row
            total = part if total is None else total + part
        return total

    rows = [(2 * TR + i, forcing[i : i + 1, :]) for i in range(TR)]
    update = jnp.where(0 < sweeps, image_update(rows), 0.0)
    z = [update[s * TR : (s + 1) * TR, :] for s in range(SECTIONS)]
    for sweep in range(1, NEWT):
        mixed = [None] * SECTIONS
        for i in range(TR):
            jac = jac_ref[i, :, lanes].astype(F32)
            for s in range(SECTIONS):
                part = jac * z[s][i : i + 1, :]
                mixed[s] = part if mixed[s] is None else mixed[s] + part
        rows = []
        for s in range(SECTIONS):
            mix = COEF[0][s] * mixed[0] + COEF[1][s] * mixed[1] + COEF[2][s] * mixed[2]
            residual = mix - z[s]
            if s == SECTIONS - 1:
                residual = residual + forcing
            rows += [(s * TR + i, residual[i : i + 1, :]) for i in range(TR)]
        update = jnp.where(sweep < sweeps, image_update(rows), 0.0)
        z = [z[s] + update[s * TR : (s + 1) * TR, :] for s in range(SECTIONS)]
    return z[0] + z[1] + z[2]


def react_kernel(
    mask_ref, slabs_ref, own_in, below_ref, above_ref, sweeps_ref, jac_ref, inv_ref,
    tiles_ref, raw_ref, own_ref, north_ref, south_ref,
):
    blocks = arrived_blocks(mask_ref, slabs_ref, own_in, below_ref, above_ref)
    blocks = [
        column_block(blocks[r], r, jac_ref, inv_ref, sweeps_ref[r : r + 1, :]) for r in range(RB)
    ]
    emit_terms(blocks, tiles_ref, raw_ref, own_ref, north_ref, south_ref)


def step_kernel(
    mask_ref, slabs_ref, own_in, below_ref, above_ref,
    tiles_ref, raw_ref, own_ref, north_ref, south_ref,
):
    blocks = arrived_blocks(mask_ref, slabs_ref, own_in, below_ref, above_ref)
    emit_terms(blocks, tiles_ref, raw_ref, own_ref, north_ref, south_ref)


def last_kernel(mask_ref, slabs_ref, own_in, below_ref, above_ref, out_ref):
    blocks = arrived_blocks(mask_ref, slabs_ref, own_in, below_ref, above_ref)
    for r in range(RB):
        out_ref[:, r * BLK : (r + 1) * BLK] = blocks[r]


def struct(*shape):
    return jax.ShapeDtypeStruct(shape, F32)


TERM_SHAPES = (
    struct(TERMS * TR, BLK),
    struct(SLAB, BLK),
    struct(SLAB, BLK),
    struct(SLAB, BLK),
)


def call(kernel, out_shape, operands, smem, name, far=0, scratch=()):
    many = isinstance(out_shape, tuple)
    size = sum(a.size * a.dtype.itemsize for a in operands)
    return pl.pallas_call(
        kernel,
        out_shape=out_shape,
        in_specs=[SMEM] * smem + [VMEM] * (len(operands) - smem - far) + [FAR] * far,
        out_specs=[VMEM] * len(out_shape) if many else VMEM,
        scratch_shapes=scratch,
        compiler_params=pltpu.CompilerParams(vmem_limit_bytes=12 * 1024 * 1024),
        cost_estimate=pl.CostEstimate(flops=0, bytes_accessed=size, transcendentals=0),
        name=name,
    )(*operands)


def body(
    adjoint,
    impl_tiles,
    expl_tiles,
    impl_dest,
    impl_local,
    expl_dest,
    expl_local,
    column_depth,
    newton,
    jacobian,
    newton_inverse,
):
    def gather_x(raw):
        return [shift_x(raw, k) for k in range(1, NX)]

    def deliver(terms, raws, slot):
        raw, own, north, south = terms
        below, above = ring_lat(north, 1), ring_lat(south, N_LAT - 1)
        *raws, below, above = lax.optimization_barrier((*raws, below, above))
        dense = struct(NZ * SLAB, BLK)
        acc = pltpu.VMEM((2 * NZ * RB + 1, TR, BLK), F32)
        mine, other = call(
            merge_kernel, (dense, dense), [slot, raw, *raws], 0, "merge", scratch=[acc, acc]
        )
        slabs = exchange_z((mine + swap_core(other)).reshape(NZ, SLAB, BLK))
        return [masks, slabs, own, below, above]

    first_shapes = (struct(TERMS * TR + 2 * RB, BLK),) + TERM_SHAPES[1:]
    terms = call(
        first_kernel,
        first_shapes,
        [
            pltpu.with_memory_space_constraint(value, pltpu.HBM)
            for value in (adjoint, impl_dest, impl_local, expl_dest, expl_local, impl_tiles)
        ],
        0,
        "first",
        far=6,
        scratch=[
            pltpu.VMEM((TR, RB * BLK), F32),
            *[pltpu.VMEM((RB, NBAND), jnp.int32)] * 4,
            pltpu.VMEM((RB, NB, BLK, BLK), jnp.bfloat16),
            pltpu.SemaphoreType.DMA((5,)),
            pltpu.SemaphoreType.DMA((RB,)),
        ],
    )
    int_table = jax.ShapeDtypeStruct((RB, BLK), jnp.int32)
    masks, sweeps = call(
        masks_kernel, (struct(RB + 2, BLK), int_table), [column_depth, newton], 2, "masks"
    )
    raws = gather_x(terms[0])
    *raws, masks, sweeps = lax.optimization_barrier((*raws, masks, sweeps))
    slot_table = jax.ShapeDtypeStruct((NX * RB, NBAND), jnp.int32)
    slots = call(slots_kernel, (slot_table, slot_table), [terms[0], *raws], 0, "slots")
    for step_index in range(STEPS):
        if step_index:
            raws = gather_x(terms[0])
        arrived = deliver(terms, raws, slots[0])
        terms = call(
            react_kernel,
            TERM_SHAPES,
            arrived + [sweeps, jacobian, newton_inverse, expl_tiles],
            0,
            "react",
        )
        arrived = deliver(terms, gather_x(terms[0]), slots[1])
        if step_index + 1 < STEPS:
            terms = call(step_kernel, TERM_SHAPES, arrived + [impl_tiles], 0, "step")
    return call(last_kernel, struct(TR, RB * BLK), arrived, 0, "last")


def solution(mesh):
    both = ("cols", "lat")
    return jax.shard_map(
        body,
        mesh=mesh,
        in_specs=(
            P(None, both),
            P(both, None, None, None),
            P(both, None, None, None),
            P(both, None),
            P(both, None),
            P(both, None),
            P(both, None),
            P(both),
            P(both),
            P(None, None, both),
            P(None, None, both),
        ),
        out_specs=P(None, both),
        check_vma=False,
    )
```

```python
import math

import jax
import jax.numpy as jnp
from jax import lax
from jax.experimental import pallas as pl
from jax.experimental.pallas import tpu as pltpu
from jax.sharding import PartitionSpec as P

NEWT = 4
STEPS = 2
TR = 10
SECTIONS = 3
BLK = 128
NBAND = 4
NB = 7
LEV = 64
RB = 4
NX, NZ, NCORE = 4, 8, 2
N_LAT = 4
TERMS = RB * NBAND
SLAB = RB * TR
F32 = jnp.float32

ROOT = math.sqrt(6.0)
COEF = [
    [(88.0 - 7.0 * ROOT) / 360.0, (296.0 - 169.0 * ROOT) / 1800.0, (-2.0 + 3.0 * ROOT) / 225.0],
    [(296.0 + 169.0 * ROOT) / 1800.0, (88.0 + 7.0 * ROOT) / 360.0, (-2.0 - 3.0 * ROOT) / 225.0],
    [(16.0 - ROOT) / 36.0, (16.0 + ROOT) / 36.0, 1.0 / 9.0],
]

VMEM = pl.BlockSpec(memory_space=pltpu.VMEM)
SMEM = pl.BlockSpec(memory_space=pltpu.SMEM)
FAR = pl.BlockSpec(memory_space=pltpu.HBM)


def cols_id(x, z, core):
    return (x * NZ + z) * NCORE + core


def shift_x(value, steps):
    pairs = [
        (cols_id(x, z, c), cols_id((x + steps) % NX, z, c))
        for x in range(NX)
        for z in range(NZ)
        for c in range(NCORE)
    ]
    return lax.ppermute(value, "cols", pairs)


def swap_core(value):
    return lax.ppermute(value, "cols", [(i, i ^ 1) for i in range(NX * NZ * NCORE)])


def ring_lat(value, steps):
    return lax.ppermute(value, "lat", [(i, (i + steps) % N_LAT) for i in range(N_LAT)])


def exchange_z(value):
    groups = [[cols_id(x, z, c) for z in range(NZ)] for x in range(NX) for c in range(NCORE)]
    return lax.all_to_all(value, "cols", 0, 0, axis_index_groups=groups, tiled=True)


def emit_terms(blocks, tiles_ref, raw_ref, own_ref, north_ref, south_ref, ready=None):
    for r in range(RB):
        if ready is not None:
            ready[r].wait()
        padded = jnp.concatenate([blocks[r], jnp.zeros((16 - TR, BLK), F32)], axis=0)
        left = padded.astype(jnp.bfloat16)
        for t in range(NB):
            term = jnp.dot(left, tiles_ref[r, t], preferred_element_type=F32)[:TR]
            if t == 0:
                own_ref[r * TR : (r + 1) * TR, :] = term
            elif t <= NBAND:
                k = r * NBAND + t - 1
                raw_ref[k * TR : (k + 1) * TR, :] = term
            elif t == NBAND + 1:
                north_ref[r * TR : (r + 1) * TR, :] = term
            else:
                south_ref[r * TR : (r + 1) * TR, :] = term


def first_kernel(
    field_far, impl_dest_far, impl_local_far, expl_dest_far, expl_local_far, tiles_far,
    raw_ref, own_ref, north_ref, south_ref,
    field_ref, impl_dest, impl_local, expl_dest, expl_local, tiles_ref, arrivals, tile_arrivals,
):
    copies = [
        pltpu.make_async_copy(far, near, arrivals.at[i])
        for i, (far, near) in enumerate(
            (
                (field_far, field_ref),
                (impl_dest_far, impl_dest),
                (impl_local_far, impl_local),
                (expl_dest_far, expl_dest),
                (expl_local_far, expl_local),
            )
        )
    ]
    tile_copies = [
        pltpu.make_async_copy(tiles_far.at[r], tiles_ref.at[r], tile_arrivals.at[r])
        for r in range(RB)
    ]
    for copy in copies + tile_copies:
        copy.start()
    raw_ref[TERMS * TR :, :] = jnp.zeros((2 * RB, BLK), F32)
    for copy in copies:
        copy.wait()
    impl_codes = impl_dest[...] * RB + impl_local[...]
    expl_codes = expl_dest[...] * RB + expl_local[...]
    raw_ref[TERMS * TR : TERMS * TR + RB, :NBAND] = impl_codes.astype(F32)
    raw_ref[TERMS * TR + RB :, :NBAND] = expl_codes.astype(F32)
    blocks = [field_ref[:, r * BLK : (r + 1) * BLK] for r in range(RB)]
    emit_terms(blocks, tiles_ref, raw_ref, own_ref, north_ref, south_ref, tile_copies)


def slots_kernel(raw0, raw1, raw2, raw3, impl_ref, expl_ref):
    cols = lax.axis_index("cols")
    my_core = cols & (NCORE - 1)
    my_x = cols // (NZ * NCORE)
    for source, raw in enumerate((raw0, raw1, raw2, raw3)):
        codes = raw[TERMS * TR :, :].astype(jnp.int32)
        owner, local = codes // RB, codes & (RB - 1)
        place = ((owner // NCORE) & (NZ - 1)) * RB + local
        place = place + jnp.where((owner & (NCORE - 1)) == my_core, 0, NZ * RB)
        slot = jnp.where(owner // (NZ * NCORE) == my_x, place, 2 * NZ * RB)
        impl_ref[source * RB : (source + 1) * RB, :] = slot[:RB, :NBAND]
        expl_ref[source * RB : (source + 1) * RB, :] = slot[RB:, :NBAND]


def masks_kernel(depth_ref, newton_ref, mask_ref, sweeps_ref):
    lat = lax.axis_index("lat")
    lane = lax.broadcasted_iota(jnp.int32, (1, BLK), 1)
    first = lane < LEV
    level = jnp.where(first, lane, lane - LEV)
    for r in range(RB):
        depth = jnp.where(first, depth_ref[2 * r], depth_ref[2 * r + 1])
        mask_ref[r : r + 1, :] = jnp.where(level < depth, 1.0, 0.0)
        sweeps_ref[r : r + 1, :] = jnp.where(first, newton_ref[2 * r], newton_ref[2 * r + 1])
    mask_ref[RB : RB + 1, :] = jnp.where(lane * 0 + lat > 0, 1.0, 0.0)
    mask_ref[RB + 1 : RB + 2, :] = jnp.where(lane * 0 + lat < N_LAT - 1, 1.0, 0.0)


def merge_kernel(slot_ref, raw0, raw1, raw2, raw3, mine_ref, other_ref, acc0, acc1):
    acc0[...] = jnp.zeros_like(acc0)
    acc1[...] = jnp.zeros_like(acc1)
    slots = slot_ref[...]
    for pair in (((0, raw0, acc0), (1, raw1, acc1)), ((2, raw2, acc0), (3, raw3, acc1))):
        for k in range(TERMS):
            for source, raw, acc in pair:
                slot = slots[source * RB + k // NBAND, k % NBAND]
                acc[slot] = acc[slot] + raw[k * TR : (k + 1) * TR, :]
    for slot in range(NZ * RB):
        mine_ref[slot * TR : (slot + 1) * TR, :] = acc0[slot] + acc1[slot]
        far = NZ * RB + slot
        other_ref[slot * TR : (slot + 1) * TR, :] = acc0[far] + acc1[far]


def arrived_blocks(mask_ref, slabs_ref, own_ref, below_ref, above_ref):
    total = own_ref[...] + below_ref[...] * mask_ref[RB : RB + 1, :]
    total = total + above_ref[...] * mask_ref[RB + 1 : RB + 2, :]
    for z in range(NZ):
        total = total + slabs_ref[z]
    return [total[r * TR : (r + 1) * TR, :] * mask_ref[r : r + 1, :] for r in range(RB)]


def column_block(forcing, r, jac_ref, inv_ref, sweeps):
    lanes = slice(r * BLK, (r + 1) * BLK)

    def image_update(rows):
        total = None
        for q, row in rows:
            part = inv_ref[q, :, lanes].astype(F32) * row
            total = part if total is None else total + part
        return total

    rows = [(2 * TR + i, forcing[i : i + 1, :]) for i in range(TR)]
    update = jnp.where(0 < sweeps, image_update(rows), 0.0)
    z = [update[s * TR : (s + 1) * TR, :] for s in range(SECTIONS)]
    for sweep in range(1, NEWT):
        mixed = [None] * SECTIONS
        for i in range(TR):
            jac = jac_ref[i, :, lanes].astype(F32)
            for s in range(SECTIONS):
                part = jac * z[s][i : i + 1, :]
                mixed[s] = part if mixed[s] is None else mixed[s] + part
        rows = []
        for s in range(SECTIONS):
            mix = COEF[0][s] * mixed[0] + COEF[1][s] * mixed[1] + COEF[2][s] * mixed[2]
            residual = mix - z[s]
            if s == SECTIONS - 1:
                residual = residual + forcing
            rows += [(s * TR + i, residual[i : i + 1, :]) for i in range(TR)]
        update = jnp.where(sweep < sweeps, image_update(rows), 0.0)
        z = [z[s] + update[s * TR : (s + 1) * TR, :] for s in range(SECTIONS)]
    return z[0] + z[1] + z[2]


def react_kernel(
    mask_ref, slabs_ref, own_in, below_ref, above_ref, sweeps_ref, jac_ref, inv_ref,
    tiles_ref, raw_ref, own_ref, north_ref, south_ref,
):
    blocks = arrived_blocks(mask_ref, slabs_ref, own_in, below_ref, above_ref)
    blocks = [
        column_block(blocks[r], r, jac_ref, inv_ref, sweeps_ref[r : r + 1, :]) for r in range(RB)
    ]
    emit_terms(blocks, tiles_ref, raw_ref, own_ref, north_ref, south_ref)


def step_kernel(
    mask_ref, slabs_ref, own_in, below_ref, above_ref,
    tiles_ref, raw_ref, own_ref, north_ref, south_ref,
):
    blocks = arrived_blocks(mask_ref, slabs_ref, own_in, below_ref, above_ref)
    emit_terms(blocks, tiles_ref, raw_ref, own_ref, north_ref, south_ref)


def last_kernel(mask_ref, slabs_ref, own_in, below_ref, above_ref, out_ref):
    blocks = arrived_blocks(mask_ref, slabs_ref, own_in, below_ref, above_ref)
    for r in range(RB):
        out_ref[:, r * BLK : (r + 1) * BLK] = blocks[r]


def struct(*shape):
    return jax.ShapeDtypeStruct(shape, F32)


TERM_SHAPES = (
    struct(TERMS * TR, BLK),
    struct(SLAB, BLK),
    struct(SLAB, BLK),
    struct(SLAB, BLK),
)


def call(kernel, out_shape, operands, smem, name, far=0, scratch=()):
    many = isinstance(out_shape, tuple)
    size = sum(a.size * a.dtype.itemsize for a in operands)
    return pl.pallas_call(
        kernel,
        out_shape=out_shape,
        in_specs=[SMEM] * smem + [VMEM] * (len(operands) - smem - far) + [FAR] * far,
        out_specs=[VMEM] * len(out_shape) if many else VMEM,
        scratch_shapes=scratch,
        compiler_params=pltpu.CompilerParams(vmem_limit_bytes=12 * 1024 * 1024),
        cost_estimate=pl.CostEstimate(flops=0, bytes_accessed=size, transcendentals=0),
        name=name,
    )(*operands)


def body(
    adjoint,
    impl_tiles,
    expl_tiles,
    impl_dest,
    impl_local,
    expl_dest,
    expl_local,
    column_depth,
    newton,
    jacobian,
    newton_inverse,
):
    def gather_x(raw):
        return [shift_x(raw, k) for k in range(1, NX)]

    def deliver(terms, raws, slot):
        raw, own, north, south = terms
        below, above = ring_lat(north, 1), ring_lat(south, N_LAT - 1)
        dense = struct(NZ * SLAB, BLK)
        acc = pltpu.VMEM((2 * NZ * RB + 1, TR, BLK), F32)
        mine, other = call(
            merge_kernel, (dense, dense), [slot, raw, *raws], 0, "merge", scratch=[acc, acc]
        )
        other, below, above = lax.optimization_barrier((other, below, above))
        slabs = exchange_z((mine + swap_core(other)).reshape(NZ, SLAB, BLK))
        return [masks, slabs, own, below, above]

    first_shapes = (struct(TERMS * TR + 2 * RB, BLK),) + TERM_SHAPES[1:]
    terms = call(
        first_kernel,
        first_shapes,
        [
            pltpu.with_memory_space_constraint(value, pltpu.HBM)
            for value in (adjoint, impl_dest, impl_local, expl_dest, expl_local, impl_tiles)
        ],
        0,
        "first",
        far=6,
        scratch=[
            pltpu.VMEM((TR, RB * BLK), F32),
            *[pltpu.VMEM((RB, NBAND), jnp.int32)] * 4,
            pltpu.VMEM((RB, NB, BLK, BLK), jnp.bfloat16),
            pltpu.SemaphoreType.DMA((5,)),
            pltpu.SemaphoreType.DMA((RB,)),
        ],
    )
    int_table = jax.ShapeDtypeStruct((RB, BLK), jnp.int32)
    masks, sweeps = call(
        masks_kernel, (struct(RB + 2, BLK), int_table), [column_depth, newton], 2, "masks"
    )
    raws = gather_x(terms[0])
    *raws, masks, sweeps = lax.optimization_barrier((*raws, masks, sweeps))
    slot_table = jax.ShapeDtypeStruct((NX * RB, NBAND), jnp.int32)
    slots = call(slots_kernel, (slot_table, slot_table), [terms[0], *raws], 0, "slots")
    for step_index in range(STEPS):
        if step_index:
            raws = gather_x(terms[0])
        arrived = deliver(terms, raws, slots[0])
        terms = call(
            react_kernel,
            TERM_SHAPES,
            arrived + [sweeps, jacobian, newton_inverse, expl_tiles],
            0,
            "react",
        )
        arrived = deliver(terms, gather_x(terms[0]), slots[1])
        if step_index + 1 < STEPS:
            terms = call(step_kernel, TERM_SHAPES, arrived + [impl_tiles], 0, "step")
    return call(last_kernel, struct(TR, RB * BLK), arrived, 0, "last")


def solution(mesh):
    both = ("cols", "lat")
    return jax.shard_map(
        body,
        mesh=mesh,
        in_specs=(
            P(None, both),
            P(both, None, None, None),
            P(both, None, None, None),
            P(both, None),
            P(both, None),
            P(both, None),
            P(both, None),
            P(both),
            P(both),
            P(None, None, both),
            P(None, None, both),
        ),
        out_specs=P(None, both),
        check_vma=False,
    )
```

```python
import math

import jax
import jax.numpy as jnp
from jax import lax
from jax.experimental import pallas as pl
from jax.experimental.pallas import tpu as pltpu
from jax.sharding import PartitionSpec as P

NEWT = 4
STEPS = 2
TR = 10
SECTIONS = 3
BLK = 128
NBAND = 4
NB = 7
LEV = 64
RB = 4
NX, NZ, NCORE = 4, 8, 2
X_SHIFTS = (1, 3, 2)
N_LAT = 4
TERMS = RB * NBAND
SLAB = RB * TR
F32 = jnp.float32

ROOT = math.sqrt(6.0)
COEF = [
    [(88.0 - 7.0 * ROOT) / 360.0, (296.0 - 169.0 * ROOT) / 1800.0, (-2.0 + 3.0 * ROOT) / 225.0],
    [(296.0 + 169.0 * ROOT) / 1800.0, (88.0 + 7.0 * ROOT) / 360.0, (-2.0 - 3.0 * ROOT) / 225.0],
    [(16.0 - ROOT) / 36.0, (16.0 + ROOT) / 36.0, 1.0 / 9.0],
]

VMEM = pl.BlockSpec(memory_space=pltpu.VMEM)
SMEM = pl.BlockSpec(memory_space=pltpu.SMEM)
FAR = pl.BlockSpec(memory_space=pltpu.HBM)


def cols_id(x, z, core):
    return (x * NZ + z) * NCORE + core


def shift_x(value, steps):
    pairs = [
        (cols_id(x, z, c), cols_id((x + steps) % NX, z, c))
        for x in range(NX)
        for z in range(NZ)
        for c in range(NCORE)
    ]
    return lax.ppermute(value, "cols", pairs)


def swap_core(value):
    return lax.ppermute(value, "cols", [(i, i ^ 1) for i in range(NX * NZ * NCORE)])


def ring_lat(value, steps):
    return lax.ppermute(value, "lat", [(i, (i + steps) % N_LAT) for i in range(N_LAT)])


def exchange_z(value):
    groups = [[cols_id(x, z, c) for z in range(NZ)] for x in range(NX) for c in range(NCORE)]
    return lax.all_to_all(value, "cols", 0, 0, axis_index_groups=groups, tiled=True)


def emit_terms(blocks, tiles_ref, raw_ref, own_ref, north_ref, south_ref, ready=None):
    for r in range(RB):
        if ready is not None:
            ready[r].wait()
        padded = jnp.concatenate([blocks[r], jnp.zeros((16 - TR, BLK), F32)], axis=0)
        left = padded.astype(jnp.bfloat16)
        for t in range(NB):
            term = jnp.dot(left, tiles_ref[r, t], preferred_element_type=F32)[:TR]
            if t == 0:
                own_ref[r * TR : (r + 1) * TR, :] = term
            elif t <= NBAND:
                k = r * NBAND + t - 1
                raw_ref[k * TR : (k + 1) * TR, :] = term
            elif t == NBAND + 1:
                north_ref[r * TR : (r + 1) * TR, :] = term
            else:
                south_ref[r * TR : (r + 1) * TR, :] = term


def start_tiles(tiles_far, tiles_ref, arrivals):
    copies = [
        pltpu.make_async_copy(tiles_far.at[r], tiles_ref.at[r], arrivals.at[r]) for r in range(RB)
    ]
    for copy in copies:
        copy.start()
    return copies


TILE_SCRATCH = [
    pltpu.VMEM((RB, NB, BLK, BLK), jnp.bfloat16),
    pltpu.SemaphoreType.DMA((RB,)),
]


def first_kernel(
    field_far, impl_dest_far, impl_local_far, expl_dest_far, expl_local_far, tiles_far,
    raw_ref, own_ref, north_ref, south_ref,
    field_ref, impl_dest, impl_local, expl_dest, expl_local, tiles_ref, tile_arrivals, arrivals,
):
    copies = [
        pltpu.make_async_copy(far, near, arrivals.at[i])
        for i, (far, near) in enumerate(
            (
                (field_far, field_ref),
                (impl_dest_far, impl_dest),
                (impl_local_far, impl_local),
                (expl_dest_far, expl_dest),
                (expl_local_far, expl_local),
            )
        )
    ]
    for copy in copies:
        copy.start()
    tile_copies = start_tiles(tiles_far, tiles_ref, tile_arrivals)
    raw_ref[TERMS * TR :, :] = jnp.zeros((2 * RB, BLK), F32)
    for copy in copies:
        copy.wait()
    impl_codes = impl_dest[...] * RB + impl_local[...]
    expl_codes = expl_dest[...] * RB + expl_local[...]
    raw_ref[TERMS * TR : TERMS * TR + RB, :NBAND] = impl_codes.astype(F32)
    raw_ref[TERMS * TR + RB :, :NBAND] = expl_codes.astype(F32)
    blocks = [field_ref[:, r * BLK : (r + 1) * BLK] for r in range(RB)]
    emit_terms(blocks, tiles_ref, raw_ref, own_ref, north_ref, south_ref, tile_copies)


def slots_kernel(raw0, raw1, raw2, raw3, impl_ref, expl_ref):
    cols = lax.axis_index("cols")
    my_core = cols & (NCORE - 1)
    my_x = cols // (NZ * NCORE)
    for source, raw in enumerate((raw0, raw1, raw2, raw3)):
        codes = raw[TERMS * TR :, :].astype(jnp.int32)
        owner, local = codes // RB, codes & (RB - 1)
        place = ((owner // NCORE) & (NZ - 1)) * RB + local
        place = place + jnp.where((owner & (NCORE - 1)) == my_core, 0, NZ * RB)
        slot = jnp.where(owner // (NZ * NCORE) == my_x, place, 2 * NZ * RB)
        impl_ref[source * RB : (source + 1) * RB, :] = slot[:RB, :NBAND]
        expl_ref[source * RB : (source + 1) * RB, :] = slot[RB:, :NBAND]


def masks_kernel(depth_ref, newton_ref, mask_ref, sweeps_ref):
    lat = lax.axis_index("lat")
    lane = lax.broadcasted_iota(jnp.int32, (1, BLK), 1)
    first = lane < LEV
    level = jnp.where(first, lane, lane - LEV)
    for r in range(RB):
        depth = jnp.where(first, depth_ref[2 * r], depth_ref[2 * r + 1])
        mask_ref[r : r + 1, :] = jnp.where(level < depth, 1.0, 0.0)
        sweeps_ref[r : r + 1, :] = jnp.where(first, newton_ref[2 * r], newton_ref[2 * r + 1])
    mask_ref[RB : RB + 1, :] = jnp.where(lane * 0 + lat > 0, 1.0, 0.0)
    mask_ref[RB + 1 : RB + 2, :] = jnp.where(lane * 0 + lat < N_LAT - 1, 1.0, 0.0)


def merge_kernel(slot_ref, raw0, raw1, raw2, raw3, mine_ref, other_ref, acc0, acc1):
    acc0[...] = jnp.zeros_like(acc0)
    acc1[...] = jnp.zeros_like(acc1)
    slots = slot_ref[...]
    for pair in (((0, raw0, acc0), (1, raw1, acc1)), ((2, raw2, acc0), (3, raw3, acc1))):
        for k in range(TERMS):
            for source, raw, acc in pair:
                slot = slots[source * RB + k // NBAND, k % NBAND]
                acc[slot] = acc[slot] + raw[k * TR : (k + 1) * TR, :]
    for slot in range(NZ * RB):
        mine_ref[slot * TR : (slot + 1) * TR, :] = acc0[slot] + acc1[slot]
        far = NZ * RB + slot
        other_ref[slot * TR : (slot + 1) * TR, :] = acc0[far] + acc1[far]


def arrived_blocks(mask_ref, slabs_ref, own_ref, below_ref, above_ref):
    total = own_ref[...] + below_ref[...] * mask_ref[RB : RB + 1, :]
    total = total + above_ref[...] * mask_ref[RB + 1 : RB + 2, :]
    for z in range(NZ):
        total = total + slabs_ref[z]
    return [total[r * TR : (r + 1) * TR, :] * mask_ref[r : r + 1, :] for r in range(RB)]


def column_block(forcing, r, jac_ref, inv_ref, sweeps):
    lanes = slice(r * BLK, (r + 1) * BLK)

    def image_update(rows):
        total = None
        for q, row in rows:
            part = inv_ref[q, :, lanes].astype(F32) * row
            total = part if total is None else total + part
        return total

    rows = [(2 * TR + i, forcing[i : i + 1, :]) for i in range(TR)]
    update = jnp.where(0 < sweeps, image_update(rows), 0.0)
    z = [update[s * TR : (s + 1) * TR, :] for s in range(SECTIONS)]
    for sweep in range(1, NEWT):
        mixed = [None] * SECTIONS
        for i in range(TR):
            jac = jac_ref[i, :, lanes].astype(F32)
            for s in range(SECTIONS):
                part = jac * z[s][i : i + 1, :]
                mixed[s] = part if mixed[s] is None else mixed[s] + part
        rows = []
        for s in range(SECTIONS):
            mix = COEF[0][s] * mixed[0] + COEF[1][s] * mixed[1] + COEF[2][s] * mixed[2]
            residual = mix - z[s]
            if s == SECTIONS - 1:
                residual = residual + forcing
            rows += [(s * TR + i, residual[i : i + 1, :]) for i in range(TR)]
        update = jnp.where(sweep < sweeps, image_update(rows), 0.0)
        z = [z[s] + update[s * TR : (s + 1) * TR, :] for s in range(SECTIONS)]
    return z[0] + z[1] + z[2]


def react_kernel(
    mask_ref, slabs_ref, own_in, below_ref, above_ref, sweeps_ref, jac_ref, inv_ref,
    tiles_far, raw_ref, own_ref, north_ref, south_ref, tiles_ref, tile_arrivals,
):
    tile_copies = start_tiles(tiles_far, tiles_ref, tile_arrivals)
    blocks = arrived_blocks(mask_ref, slabs_ref, own_in, below_ref, above_ref)
    blocks = [
        column_block(blocks[r], r, jac_ref, inv_ref, sweeps_ref[r : r + 1, :]) for r in range(RB)
    ]
    emit_terms(blocks, tiles_ref, raw_ref, own_ref, north_ref, south_ref, tile_copies)


def step_kernel(
    mask_ref, slabs_ref, own_in, below_ref, above_ref,
    tiles_ref, raw_ref, own_ref, north_ref, south_ref,
):
    blocks = arrived_blocks(mask_ref, slabs_ref, own_in, below_ref, above_ref)
    emit_terms(blocks, tiles_ref, raw_ref, own_ref, north_ref, south_ref)


def last_kernel(mask_ref, slabs_ref, own_in, below_ref, above_ref, out_ref):
    blocks = arrived_blocks(mask_ref, slabs_ref, own_in, below_ref, above_ref)
    for r in range(RB):
        out_ref[:, r * BLK : (r + 1) * BLK] = blocks[r]


def struct(*shape):
    return jax.ShapeDtypeStruct(shape, F32)


TERM_SHAPES = (
    struct(TERMS * TR, BLK),
    struct(SLAB, BLK),
    struct(SLAB, BLK),
    struct(SLAB, BLK),
)


def call(kernel, out_shape, operands, smem, name, far=0, scratch=()):
    many = isinstance(out_shape, tuple)
    size = sum(a.size * a.dtype.itemsize for a in operands)
    return pl.pallas_call(
        kernel,
        out_shape=out_shape,
        in_specs=[SMEM] * smem + [VMEM] * (len(operands) - smem - far) + [FAR] * far,
        out_specs=[VMEM] * len(out_shape) if many else VMEM,
        scratch_shapes=scratch,
        compiler_params=pltpu.CompilerParams(vmem_limit_bytes=12 * 1024 * 1024),
        cost_estimate=pl.CostEstimate(flops=0, bytes_accessed=size, transcendentals=0),
        name=name,
    )(*operands)


def body(
    adjoint,
    impl_tiles,
    expl_tiles,
    impl_dest,
    impl_local,
    expl_dest,
    expl_local,
    column_depth,
    newton,
    jacobian,
    newton_inverse,
):
    def gather_x(raw):
        return [shift_x(raw, k) for k in X_SHIFTS]

    def deliver(terms, raws, slot):
        raw, own, north, south = terms
        below, above = ring_lat(north, 1), ring_lat(south, N_LAT - 1)
        dense = struct(NZ * SLAB, BLK)
        acc = pltpu.VMEM((2 * NZ * RB + 1, TR, BLK), F32)
        mine, other = call(
            merge_kernel, (dense, dense), [slot, raw, *raws], 0, "merge", scratch=[acc, acc]
        )
        other, below, above = lax.optimization_barrier((other, below, above))
        slabs = exchange_z((mine + swap_core(other)).reshape(NZ, SLAB, BLK))
        return [masks, slabs, own, below, above]

    first_shapes = (struct(TERMS * TR + 2 * RB, BLK),) + TERM_SHAPES[1:]
    terms = call(
        first_kernel,
        first_shapes,
        [
            pltpu.with_memory_space_constraint(value, pltpu.HBM)
            for value in (adjoint, impl_dest, impl_local, expl_dest, expl_local, impl_tiles)
        ],
        0,
        "first",
        far=6,
        scratch=[
            pltpu.VMEM((TR, RB * BLK), F32),
            *[pltpu.VMEM((RB, NBAND), jnp.int32)] * 4,
            *TILE_SCRATCH,
            pltpu.SemaphoreType.DMA((5,)),
        ],
    )
    int_table = jax.ShapeDtypeStruct((RB, BLK), jnp.int32)
    masks, sweeps = call(
        masks_kernel, (struct(RB + 2, BLK), int_table), [column_depth, newton], 2, "masks"
    )
    raws = gather_x(terms[0])
    *raws, masks, sweeps = lax.optimization_barrier((*raws, masks, sweeps))
    slot_table = jax.ShapeDtypeStruct((NX * RB, NBAND), jnp.int32)
    slots = call(slots_kernel, (slot_table, slot_table), [terms[0], *raws], 0, "slots")
    expl_far = pltpu.with_memory_space_constraint(expl_tiles, pltpu.HBM)
    for step_index in range(STEPS):
        if step_index:
            raws = gather_x(terms[0])
        arrived = deliver(terms, raws, slots[0])
        terms = call(
            react_kernel,
            TERM_SHAPES,
            arrived + [sweeps, jacobian, newton_inverse, expl_far],
            0,
            "react",
            far=1,
            scratch=TILE_SCRATCH,
        )
        arrived = deliver(terms, gather_x(terms[0]), slots[1])
        if step_index + 1 < STEPS:
            terms = call(step_kernel, TERM_SHAPES, arrived + [impl_tiles], 0, "step")
    return call(last_kernel, struct(TR, RB * BLK), arrived, 0, "last")


def solution(mesh):
    both = ("cols", "lat")
    return jax.shard_map(
        body,
        mesh=mesh,
        in_specs=(
            P(None, both),
            P(both, None, None, None),
            P(both, None, None, None),
            P(both, None),
            P(both, None),
            P(both, None),
            P(both, None),
            P(both),
            P(both),
            P(None, None, both),
            P(None, None, both),
        ),
        out_specs=P(None, both),
        check_vma=False,
    )
```

```python
import math

import jax
import jax.numpy as jnp
from jax import lax
from jax.experimental import pallas as pl
from jax.experimental.pallas import tpu as pltpu
from jax.sharding import PartitionSpec as P

NEWT = 4
STEPS = 2
TR = 10
SECTIONS = 3
BLK = 128
NBAND = 4
NB = 7
LEV = 64
RB = 4
NX, NZ, NCORE = 4, 8, 2
N_LAT = 4
TERMS = RB * NBAND
SLAB = RB * TR
F32 = jnp.float32

ROOT = math.sqrt(6.0)
COEF = [
    [(88.0 - 7.0 * ROOT) / 360.0, (296.0 - 169.0 * ROOT) / 1800.0, (-2.0 + 3.0 * ROOT) / 225.0],
    [(296.0 + 169.0 * ROOT) / 1800.0, (88.0 + 7.0 * ROOT) / 360.0, (-2.0 - 3.0 * ROOT) / 225.0],
    [(16.0 - ROOT) / 36.0, (16.0 + ROOT) / 36.0, 1.0 / 9.0],
]

VMEM = pl.BlockSpec(memory_space=pltpu.VMEM)
SMEM = pl.BlockSpec(memory_space=pltpu.SMEM)
FAR = pl.BlockSpec(memory_space=pltpu.HBM)


def cols_id(x, z, core):
    return (x * NZ + z) * NCORE + core


def shift_x(value, steps):
    pairs = [
        (cols_id(x, z, c), cols_id((x + steps) % NX, z, c))
        for x in range(NX)
        for z in range(NZ)
        for c in range(NCORE)
    ]
    return lax.ppermute(value, "cols", pairs)


def swap_core(value):
    return lax.ppermute(value, "cols", [(i, i ^ 1) for i in range(NX * NZ * NCORE)])


def ring_lat(value, steps):
    return lax.ppermute(value, "lat", [(i, (i + steps) % N_LAT) for i in range(N_LAT)])


def exchange_z(value):
    groups = [[cols_id(x, z, c) for z in range(NZ)] for x in range(NX) for c in range(NCORE)]
    return lax.all_to_all(value, "cols", 0, 0, axis_index_groups=groups, tiled=True)


def emit_terms(blocks, tiles_ref, raw_ref, own_ref, north_ref, south_ref, ready=None):
    for r in range(RB):
        for copy in ready[r] if ready else ():
            copy.wait()
        padded = jnp.concatenate([blocks[r], jnp.zeros((16 - TR, BLK), F32)], axis=0)
        left = padded.astype(jnp.bfloat16)
        for t in range(NB):
            term = jnp.dot(left, tiles_ref[r, t], preferred_element_type=F32)[:TR]
            if t == 0:
                own_ref[r * TR : (r + 1) * TR, :] = term
            elif t <= NBAND:
                k = r * NBAND + t - 1
                raw_ref[k * TR : (k + 1) * TR, :] = term
            elif t == NBAND + 1:
                north_ref[r * TR : (r + 1) * TR, :] = term
            else:
                south_ref[r * TR : (r + 1) * TR, :] = term


def first_kernel(
    field_far, impl_dest_far, impl_local_far, expl_dest_far, expl_local_far, depth_far, newton_far,
    tiles_far,
    raw_ref, own_ref, north_ref, south_ref, mask_ref, sweeps_ref,
    field_ref, impl_dest, impl_local, expl_dest, expl_local, depth_ref, newton_ref,
    tiles_ref, arrivals, tile_arrivals,
):
    copies = [
        pltpu.make_async_copy(far, near, arrivals.at[i])
        for i, (far, near) in enumerate(
            (
                (field_far, field_ref),
                (impl_dest_far, impl_dest),
                (impl_local_far, impl_local),
                (expl_dest_far, expl_dest),
                (expl_local_far, expl_local),
                (depth_far, depth_ref),
                (newton_far, newton_ref),
            )
        )
    ]
    tile_copies = [
        [
            pltpu.make_async_copy(tiles_far.at[r, t], tiles_ref.at[r, t], tile_arrivals.at[r, t])
            for t in range(NB)
        ]
        for r in range(RB)
    ]
    for copy in copies:
        copy.start()
    for row in tile_copies:
        for copy in row:
            copy.start()
    raw_ref[TERMS * TR :, :] = jnp.zeros((2 * RB, BLK), F32)
    for copy in copies:
        copy.wait()
    impl_codes = impl_dest[...] * RB + impl_local[...]
    expl_codes = expl_dest[...] * RB + expl_local[...]
    raw_ref[TERMS * TR : TERMS * TR + RB, :NBAND] = impl_codes.astype(F32)
    raw_ref[TERMS * TR + RB :, :NBAND] = expl_codes.astype(F32)
    write_masks(depth_ref, newton_ref, mask_ref, sweeps_ref)
    blocks = [field_ref[:, r * BLK : (r + 1) * BLK] for r in range(RB)]
    emit_terms(blocks, tiles_ref, raw_ref, own_ref, north_ref, south_ref, tile_copies)


def slots_kernel(raw0, raw1, raw2, raw3, impl_ref, expl_ref):
    cols = lax.axis_index("cols")
    my_core = cols & (NCORE - 1)
    my_x = cols // (NZ * NCORE)
    for source, raw in enumerate((raw0, raw1, raw2, raw3)):
        codes = raw[TERMS * TR :, :].astype(jnp.int32)
        owner, local = codes // RB, codes & (RB - 1)
        place = ((owner // NCORE) & (NZ - 1)) * RB + local
        place = place + jnp.where((owner & (NCORE - 1)) == my_core, 0, NZ * RB)
        slot = jnp.where(owner // (NZ * NCORE) == my_x, place, 2 * NZ * RB)
        impl_ref[source * RB : (source + 1) * RB, :] = slot[:RB, :NBAND]
        expl_ref[source * RB : (source + 1) * RB, :] = slot[RB:, :NBAND]


def write_masks(depth_ref, newton_ref, mask_ref, sweeps_ref):
    lat = lax.axis_index("lat")
    lane = lax.broadcasted_iota(jnp.int32, (1, BLK), 1)
    first = lane < LEV
    level = jnp.where(first, lane, lane - LEV)
    for r in range(RB):
        depth = jnp.where(first, depth_ref[2 * r], depth_ref[2 * r + 1])
        mask_ref[r : r + 1, :] = jnp.where(level < depth, 1.0, 0.0)
        sweeps_ref[r : r + 1, :] = jnp.where(first, newton_ref[2 * r], newton_ref[2 * r + 1])
    mask_ref[RB : RB + 1, :] = jnp.where(lane * 0 + lat > 0, 1.0, 0.0)
    mask_ref[RB + 1 : RB + 2, :] = jnp.where(lane * 0 + lat < N_LAT - 1, 1.0, 0.0)


def merge_kernel(slot_ref, raw0, raw1, raw2, raw3, mine_ref, other_ref, acc0, acc1):
    acc0[...] = jnp.zeros_like(acc0)
    acc1[...] = jnp.zeros_like(acc1)
    slots = slot_ref[...]
    for pair in (((0, raw0, acc0), (1, raw1, acc1)), ((2, raw2, acc0), (3, raw3, acc1))):
        for k in range(TERMS):
            for source, raw, acc in pair:
                slot = slots[source * RB + k // NBAND, k % NBAND]
                acc[slot] = acc[slot] + raw[k * TR : (k + 1) * TR, :]
    for slot in range(NZ * RB):
        mine_ref[slot * TR : (slot + 1) * TR, :] = acc0[slot] + acc1[slot]
        far = NZ * RB + slot
        other_ref[slot * TR : (slot + 1) * TR, :] = acc0[far] + acc1[far]


def arrived_blocks(mask_ref, slabs_ref, own_ref, below_ref, above_ref):
    total = own_ref[...] + below_ref[...] * mask_ref[RB : RB + 1, :]
    total = total + above_ref[...] * mask_ref[RB + 1 : RB + 2, :]
    for z in range(NZ):
        total = total + slabs_ref[z]
    return [total[r * TR : (r + 1) * TR, :] * mask_ref[r : r + 1, :] for r in range(RB)]


def column_block(forcing, r, jac_ref, inv_ref, sweeps):
    lanes = slice(r * BLK, (r + 1) * BLK)

    def image_update(rows):
        total = None
        for q, row in rows:
            part = inv_ref[q, :, lanes].astype(F32) * row
            total = part if total is None else total + part
        return total

    rows = [(2 * TR + i, forcing[i : i + 1, :]) for i in range(TR)]
    update = jnp.where(0 < sweeps, image_update(rows), 0.0)
    z = [update[s * TR : (s + 1) * TR, :] for s in range(SECTIONS)]
    for sweep in range(1, NEWT):
        mixed = [None] * SECTIONS
        for i in range(TR):
            jac = jac_ref[i, :, lanes].astype(F32)
            for s in range(SECTIONS):
                part = jac * z[s][i : i + 1, :]
                mixed[s] = part if mixed[s] is None else mixed[s] + part
        rows = []
        for s in range(SECTIONS):
            mix = COEF[0][s] * mixed[0] + COEF[1][s] * mixed[1] + COEF[2][s] * mixed[2]
            residual = mix - z[s]
            if s == SECTIONS - 1:
                residual = residual + forcing
            rows += [(s * TR + i, residual[i : i + 1, :]) for i in range(TR)]
        update = jnp.where(sweep < sweeps, image_update(rows), 0.0)
        z = [z[s] + update[s * TR : (s + 1) * TR, :] for s in range(SECTIONS)]
    return z[0] + z[1] + z[2]


def react_kernel(
    mask_ref, slabs_ref, own_in, below_ref, above_ref, sweeps_ref, jac_ref, inv_ref,
    tiles_ref, raw_ref, own_ref, north_ref, south_ref,
):
    blocks = arrived_blocks(mask_ref, slabs_ref, own_in, below_ref, above_ref)
    blocks = [
        column_block(blocks[r], r, jac_ref, inv_ref, sweeps_ref[r : r + 1, :]) for r in range(RB)
    ]
    emit_terms(blocks, tiles_ref, raw_ref, own_ref, north_ref, south_ref)


def step_kernel(
    mask_ref, slabs_ref, own_in, below_ref, above_ref,
    tiles_ref, raw_ref, own_ref, north_ref, south_ref,
):
    blocks = arrived_blocks(mask_ref, slabs_ref, own_in, below_ref, above_ref)
    emit_terms(blocks, tiles_ref, raw_ref, own_ref, north_ref, south_ref)


def last_kernel(mask_ref, slabs_ref, own_in, below_ref, above_ref, out_ref):
    blocks = arrived_blocks(mask_ref, slabs_ref, own_in, below_ref, above_ref)
    for r in range(RB):
        out_ref[:, r * BLK : (r + 1) * BLK] = blocks[r]


def struct(*shape):
    return jax.ShapeDtypeStruct(shape, F32)


TERM_SHAPES = (
    struct(TERMS * TR, BLK),
    struct(SLAB, BLK),
    struct(SLAB, BLK),
    struct(SLAB, BLK),
)


def call(kernel, out_shape, operands, smem, name, far=0, scratch=()):
    many = isinstance(out_shape, tuple)
    size = sum(a.size * a.dtype.itemsize for a in operands)
    return pl.pallas_call(
        kernel,
        out_shape=out_shape,
        in_specs=[SMEM] * smem + [VMEM] * (len(operands) - smem - far) + [FAR] * far,
        out_specs=[VMEM] * len(out_shape) if many else VMEM,
        scratch_shapes=scratch,
        compiler_params=pltpu.CompilerParams(vmem_limit_bytes=12 * 1024 * 1024),
        cost_estimate=pl.CostEstimate(flops=0, bytes_accessed=size, transcendentals=0),
        name=name,
    )(*operands)


def body(
    adjoint,
    impl_tiles,
    expl_tiles,
    impl_dest,
    impl_local,
    expl_dest,
    expl_local,
    column_depth,
    newton,
    jacobian,
    newton_inverse,
):
    def gather_x(raw):
        return [shift_x(raw, k) for k in range(1, NX)]

    def deliver(terms, raws, slot):
        raw, own, north, south = terms
        below, above = ring_lat(north, 1), ring_lat(south, N_LAT - 1)
        dense = struct(NZ * SLAB, BLK)
        acc = pltpu.VMEM((2 * NZ * RB + 1, TR, BLK), F32)
        mine, other = call(
            merge_kernel, (dense, dense), [slot, raw, *raws], 0, "merge", scratch=[acc, acc]
        )
        other, below, above = lax.optimization_barrier((other, below, above))
        slabs = exchange_z((mine + swap_core(other)).reshape(NZ, SLAB, BLK))
        return [masks, slabs, own, below, above]

    far_inputs = (adjoint, impl_dest, impl_local, expl_dest, expl_local)
    far_inputs += (column_depth, newton, impl_tiles)
    first_shapes = (struct(TERMS * TR + 2 * RB, BLK),) + TERM_SHAPES[1:] + (
        struct(RB + 2, BLK),
        jax.ShapeDtypeStruct((RB, BLK), jnp.int32),
    )
    raw, own, north, south, masks, sweeps = call(
        first_kernel,
        first_shapes,
        [
            pltpu.with_memory_space_constraint(value, pltpu.HBM)
            for value in far_inputs
        ],
        0,
        "first",
        far=8,
        scratch=[
            pltpu.VMEM((TR, RB * BLK), F32),
            *[pltpu.VMEM((RB, NBAND), jnp.int32)] * 4,
            *[pltpu.SMEM((RB * BLK // LEV,), jnp.int32)] * 2,
            pltpu.VMEM((RB, NB, BLK, BLK), jnp.bfloat16),
            pltpu.SemaphoreType.DMA((7,)),
            pltpu.SemaphoreType.DMA((RB, NB)),
        ],
    )
    raws = gather_x(raw)
    slot_table = jax.ShapeDtypeStruct((NX * RB, NBAND), jnp.int32)
    terms = (raw, own, north, south)
    slots = call(slots_kernel, (slot_table, slot_table), [raw, *raws], 0, "slots")
    for step_index in range(STEPS):
        if step_index:
            raws = gather_x(terms[0])
        arrived = deliver(terms, raws, slots[0])
        terms = call(
            react_kernel,
            TERM_SHAPES,
            arrived + [sweeps, jacobian, newton_inverse, expl_tiles],
            0,
            "react",
        )
        arrived = deliver(terms, gather_x(terms[0]), slots[1])
        if step_index + 1 < STEPS:
            terms = call(step_kernel, TERM_SHAPES, arrived + [impl_tiles], 0, "step")
    return call(last_kernel, struct(TR, RB * BLK), arrived, 0, "last")


def solution(mesh):
    both = ("cols", "lat")
    return jax.shard_map(
        body,
        mesh=mesh,
        in_specs=(
            P(None, both),
            P(both, None, None, None),
            P(both, None, None, None),
            P(both, None),
            P(both, None),
            P(both, None),
            P(both, None),
            P(both),
            P(both),
            P(None, None, both),
            P(None, None, both),
        ),
        out_specs=P(None, both),
        check_vma=False,
    )
```

```python
import math

import jax
import jax.numpy as jnp
from jax import lax
from jax.experimental import pallas as pl
from jax.experimental.pallas import tpu as pltpu
from jax.sharding import PartitionSpec as P

NEWT = 4
STEPS = 2
TR = 10
SECTIONS = 3
BLK = 128
NBAND = 4
NB = 7
LEV = 64
RB = 4
NX, NZ, NCORE = 4, 8, 2
N_LAT = 4
TERMS = RB * NBAND
SLAB = RB * TR
F32 = jnp.float32

ROOT = math.sqrt(6.0)
COEF = [
    [(88.0 - 7.0 * ROOT) / 360.0, (296.0 - 169.0 * ROOT) / 1800.0, (-2.0 + 3.0 * ROOT) / 225.0],
    [(296.0 + 169.0 * ROOT) / 1800.0, (88.0 + 7.0 * ROOT) / 360.0, (-2.0 - 3.0 * ROOT) / 225.0],
    [(16.0 - ROOT) / 36.0, (16.0 + ROOT) / 36.0, 1.0 / 9.0],
]

VMEM = pl.BlockSpec(memory_space=pltpu.VMEM)
SMEM = pl.BlockSpec(memory_space=pltpu.SMEM)
FAR = pl.BlockSpec(memory_space=pltpu.HBM)


def cols_id(x, z, core):
    return (x * NZ + z) * NCORE + core


def shift_x(value, steps):
    pairs = [
        (cols_id(x, z, c), cols_id((x + steps) % NX, z, c))
        for x in range(NX)
        for z in range(NZ)
        for c in range(NCORE)
    ]
    return lax.ppermute(value, "cols", pairs)


def swap_core(value):
    return lax.ppermute(value, "cols", [(i, i ^ 1) for i in range(NX * NZ * NCORE)])


def ring_lat(value, steps):
    return lax.ppermute(value, "lat", [(i, (i + steps) % N_LAT) for i in range(N_LAT)])


def exchange_z(value):
    groups = [[cols_id(x, z, c) for z in range(NZ)] for x in range(NX) for c in range(NCORE)]
    return lax.all_to_all(value, "cols", 0, 0, axis_index_groups=groups, tiled=True)


def emit_terms(blocks, tiles_ref, raw_ref, own_ref, north_ref, south_ref, ready=None):
    for r in range(RB):
        if ready is not None:
            ready[r].wait()
        padded = jnp.concatenate([blocks[r], jnp.zeros((16 - TR, BLK), F32)], axis=0)
        left = padded.astype(jnp.bfloat16)
        for t in range(NB):
            term = jnp.dot(left, tiles_ref[r, t], preferred_element_type=F32)[:TR]
            if t == 0:
                own_ref[r * TR : (r + 1) * TR, :] = term
            elif t <= NBAND:
                k = r * NBAND + t - 1
                raw_ref[k * TR : (k + 1) * TR, :] = term
            elif t == NBAND + 1:
                north_ref[r * TR : (r + 1) * TR, :] = term
            else:
                south_ref[r * TR : (r + 1) * TR, :] = term


def first_kernel(
    field_far, impl_dest_far, impl_local_far, expl_dest_far, expl_local_far, depth_far, newton_far,
    tiles_far,
    raw_ref, own_ref, north_ref, south_ref, mask_ref, sweeps_ref,
    field_ref, impl_dest, impl_local, expl_dest, expl_local, depth_ref, newton_ref,
    tiles_ref, arrivals, tile_arrivals,
):
    copies = [
        pltpu.make_async_copy(far, near, arrivals.at[i])
        for i, (far, near) in enumerate(
            (
                (field_far, field_ref),
                (impl_dest_far, impl_dest),
                (impl_local_far, impl_local),
                (expl_dest_far, expl_dest),
                (expl_local_far, expl_local),
                (depth_far, depth_ref),
                (newton_far, newton_ref),
            )
        )
    ]
    tile_copies = [
        pltpu.make_async_copy(tiles_far.at[r], tiles_ref.at[r], tile_arrivals.at[r])
        for r in range(RB)
    ]
    for copy in tile_copies[:1] + copies + tile_copies[1:]:
        copy.start()
    raw_ref[TERMS * TR :, :] = jnp.zeros((2 * RB, BLK), F32)
    for copy in copies:
        copy.wait()
    impl_codes = impl_dest[...] * RB + impl_local[...]
    expl_codes = expl_dest[...] * RB + expl_local[...]
    raw_ref[TERMS * TR : TERMS * TR + RB, :NBAND] = impl_codes.astype(F32)
    raw_ref[TERMS * TR + RB :, :NBAND] = expl_codes.astype(F32)
    write_masks(depth_ref, newton_ref, mask_ref, sweeps_ref)
    blocks = [field_ref[:, r * BLK : (r + 1) * BLK] for r in range(RB)]
    emit_terms(blocks, tiles_ref, raw_ref, own_ref, north_ref, south_ref, tile_copies)


def slots_kernel(raw0, raw1, raw2, raw3, impl_ref, expl_ref):
    cols = lax.axis_index("cols")
    my_core = cols & (NCORE - 1)
    my_x = cols // (NZ * NCORE)
    for source, raw in enumerate((raw0, raw1, raw2, raw3)):
        codes = raw[TERMS * TR :, :].astype(jnp.int32)
        owner, local = codes // RB, codes & (RB - 1)
        place = ((owner // NCORE) & (NZ - 1)) * RB + local
        place = place + jnp.where((owner & (NCORE - 1)) == my_core, 0, NZ * RB)
        slot = jnp.where(owner // (NZ * NCORE) == my_x, place, 2 * NZ * RB)
        impl_ref[source * RB : (source + 1) * RB, :] = slot[:RB, :NBAND]
        expl_ref[source * RB : (source + 1) * RB, :] = slot[RB:, :NBAND]


def write_masks(depth_ref, newton_ref, mask_ref, sweeps_ref):
    lat = lax.axis_index("lat")
    lane = lax.broadcasted_iota(jnp.int32, (1, BLK), 1)
    first = lane < LEV
    level = jnp.where(first, lane, lane - LEV)
    for r in range(RB):
        depth = jnp.where(first, depth_ref[2 * r], depth_ref[2 * r + 1])
        mask_ref[r : r + 1, :] = jnp.where(level < depth, 1.0, 0.0)
        sweeps_ref[r : r + 1, :] = jnp.where(first, newton_ref[2 * r], newton_ref[2 * r + 1])
    mask_ref[RB : RB + 1, :] = jnp.where(lane * 0 + lat > 0, 1.0, 0.0)
    mask_ref[RB + 1 : RB + 2, :] = jnp.where(lane * 0 + lat < N_LAT - 1, 1.0, 0.0)


def merge_kernel(slot_ref, raw0, raw1, raw2, raw3, mine_ref, other_ref, acc0, acc1):
    acc0[...] = jnp.zeros_like(acc0)
    acc1[...] = jnp.zeros_like(acc1)
    slots = slot_ref[...]
    for pair in (((0, raw0, acc0), (1, raw1, acc1)), ((2, raw2, acc0), (3, raw3, acc1))):
        for k in range(TERMS):
            for source, raw, acc in pair:
                slot = slots[source * RB + k // NBAND, k % NBAND]
                acc[slot] = acc[slot] + raw[k * TR : (k + 1) * TR, :]
    for slot in range(NZ * RB):
        mine_ref[slot * TR : (slot + 1) * TR, :] = acc0[slot] + acc1[slot]
        far = NZ * RB + slot
        other_ref[slot * TR : (slot + 1) * TR, :] = acc0[far] + acc1[far]


def arrived_blocks(mask_ref, slabs_ref, own_ref, below_ref, above_ref):
    total = own_ref[...] + below_ref[...] * mask_ref[RB : RB + 1, :]
    total = total + above_ref[...] * mask_ref[RB + 1 : RB + 2, :]
    for z in range(NZ):
        total = total + slabs_ref[z]
    return [total[r * TR : (r + 1) * TR, :] * mask_ref[r : r + 1, :] for r in range(RB)]


def column_block(forcing, r, jac_ref, inv_ref, sweeps):
    lanes = slice(r * BLK, (r + 1) * BLK)

    def image_update(rows):
        total = None
        for q, row in rows:
            part = inv_ref[q, :, lanes].astype(F32) * row
            total = part if total is None else total + part
        return total

    rows = [(2 * TR + i, forcing[i : i + 1, :]) for i in range(TR)]
    update = jnp.where(0 < sweeps, image_update(rows), 0.0)
    z = [update[s * TR : (s + 1) * TR, :] for s in range(SECTIONS)]
    for sweep in range(1, NEWT):
        mixed = [None] * SECTIONS
        for i in range(TR):
            jac = jac_ref[i, :, lanes].astype(F32)
            for s in range(SECTIONS):
                part = jac * z[s][i : i + 1, :]
                mixed[s] = part if mixed[s] is None else mixed[s] + part
        rows = []
        for s in range(SECTIONS):
            mix = COEF[0][s] * mixed[0] + COEF[1][s] * mixed[1] + COEF[2][s] * mixed[2]
            residual = mix - z[s]
            if s == SECTIONS - 1:
                residual = residual + forcing
            rows += [(s * TR + i, residual[i : i + 1, :]) for i in range(TR)]
        update = jnp.where(sweep < sweeps, image_update(rows), 0.0)
        z = [z[s] + update[s * TR : (s + 1) * TR, :] for s in range(SECTIONS)]
    return z[0] + z[1] + z[2]


def react_kernel(
    mask_ref, slabs_ref, own_in, below_ref, above_ref, sweeps_ref, jac_ref, inv_ref,
    tiles_ref, raw_ref, own_ref, north_ref, south_ref,
):
    blocks = arrived_blocks(mask_ref, slabs_ref, own_in, below_ref, above_ref)
    blocks = [
        column_block(blocks[r], r, jac_ref, inv_ref, sweeps_ref[r : r + 1, :]) for r in range(RB)
    ]
    emit_terms(blocks, tiles_ref, raw_ref, own_ref, north_ref, south_ref)


def step_kernel(
    mask_ref, slabs_ref, own_in, below_ref, above_ref,
    tiles_ref, raw_ref, own_ref, north_ref, south_ref,
):
    blocks = arrived_blocks(mask_ref, slabs_ref, own_in, below_ref, above_ref)
    emit_terms(blocks, tiles_ref, raw_ref, own_ref, north_ref, south_ref)


def last_kernel(mask_ref, slabs_ref, own_in, below_ref, above_ref, out_ref):
    blocks = arrived_blocks(mask_ref, slabs_ref, own_in, below_ref, above_ref)
    for r in range(RB):
        out_ref[:, r * BLK : (r + 1) * BLK] = blocks[r]


def struct(*shape):
    return jax.ShapeDtypeStruct(shape, F32)


TERM_SHAPES = (
    struct(TERMS * TR, BLK),
    struct(SLAB, BLK),
    struct(SLAB, BLK),
    struct(SLAB, BLK),
)


def call(kernel, out_shape, operands, smem, name, far=0, scratch=()):
    many = isinstance(out_shape, tuple)
    size = sum(a.size * a.dtype.itemsize for a in operands)
    return pl.pallas_call(
        kernel,
        out_shape=out_shape,
        in_specs=[SMEM] * smem + [VMEM] * (len(operands) - smem - far) + [FAR] * far,
        out_specs=[VMEM] * len(out_shape) if many else VMEM,
        scratch_shapes=scratch,
        compiler_params=pltpu.CompilerParams(vmem_limit_bytes=12 * 1024 * 1024),
        cost_estimate=pl.CostEstimate(flops=0, bytes_accessed=size, transcendentals=0),
        name=name,
    )(*operands)


def body(
    adjoint,
    impl_tiles,
    expl_tiles,
    impl_dest,
    impl_local,
    expl_dest,
    expl_local,
    column_depth,
    newton,
    jacobian,
    newton_inverse,
):
    def gather_x(raw):
        return [shift_x(raw, k) for k in range(1, NX)]

    def deliver(terms, raws, slot):
        raw, own, north, south = terms
        below, above = ring_lat(north, 1), ring_lat(south, N_LAT - 1)
        dense = struct(NZ * SLAB, BLK)
        acc = pltpu.VMEM((2 * NZ * RB + 1, TR, BLK), F32)
        mine, other = call(
            merge_kernel, (dense, dense), [slot, raw, *raws], 0, "merge", scratch=[acc, acc]
        )
        other, below, above = lax.optimization_barrier((other, below, above))
        slabs = exchange_z((mine + swap_core(other)).reshape(NZ, SLAB, BLK))
        return [masks, slabs, own, below, above]

    far_inputs = (adjoint, impl_dest, impl_local, expl_dest, expl_local)
    far_inputs += (column_depth, newton, impl_tiles)
    first_shapes = (struct(TERMS * TR + 2 * RB, BLK),) + TERM_SHAPES[1:] + (
        struct(RB + 2, BLK),
        jax.ShapeDtypeStruct((RB, BLK), jnp.int32),
    )
    raw, own, north, south, masks, sweeps = call(
        first_kernel,
        first_shapes,
        [
            pltpu.with_memory_space_constraint(value, pltpu.HBM)
            for value in far_inputs
        ],
        0,
        "first",
        far=8,
        scratch=[
            pltpu.VMEM((TR, RB * BLK), F32),
            *[pltpu.VMEM((RB, NBAND), jnp.int32)] * 4,
            *[pltpu.SMEM((RB * BLK // LEV,), jnp.int32)] * 2,
            pltpu.VMEM((RB, NB, BLK, BLK), jnp.bfloat16),
            pltpu.SemaphoreType.DMA((7,)),
            pltpu.SemaphoreType.DMA((RB,)),
        ],
    )
    raws = gather_x(raw)
    slot_table = jax.ShapeDtypeStruct((NX * RB, NBAND), jnp.int32)
    terms = (raw, own, north, south)
    slots = call(slots_kernel, (slot_table, slot_table), [raw, *raws], 0, "slots")
    for step_index in range(STEPS):
        if step_index:
            raws = gather_x(terms[0])
        arrived = deliver(terms, raws, slots[0])
        terms = call(
            react_kernel,
            TERM_SHAPES,
            arrived + [sweeps, jacobian, newton_inverse, expl_tiles],
            0,
            "react",
        )
        arrived = deliver(terms, gather_x(terms[0]), slots[1])
        if step_index + 1 < STEPS:
            terms = call(step_kernel, TERM_SHAPES, arrived + [impl_tiles], 0, "step")
    return call(last_kernel, struct(TR, RB * BLK), arrived, 0, "last")


def solution(mesh):
    both = ("cols", "lat")
    return jax.shard_map(
        body,
        mesh=mesh,
        in_specs=(
            P(None, both),
            P(both, None, None, None),
            P(both, None, None, None),
            P(both, None),
            P(both, None),
            P(both, None),
            P(both, None),
            P(both),
            P(both),
            P(None, None, both),
            P(None, None, both),
        ),
        out_specs=P(None, both),
        check_vma=False,
    )
```
